256 devices in a mesh: branch: 2 (over core), seq: 16 (over z, y_hi), fsdp: 8 (over y_lo, x).
Axes of the slice: x: 4, y: 4 (y_hi: 2, y_lo: 2; y = y_hi * 2 + y_lo), z: 8, core: 2. Of those that a mesh axis runs over, the one named last changes fastest.
Arguments:
- latents: bfloat16 [3072, 5120], P('seq'), may hold values from -6 to 6
- noise: bfloat16 [2, 3072, 5120], P(None, 'seq'), may hold values from -6 to 6
- time_index: int32 [2], replicated, may hold values from 20 to 979
- cfg_pair: int32 [2], replicated, may hold values from 0 to 15
- cond_table: float32 [16, 5120], replicated, may hold values from -6 to 6
- gain: float32 [2, 5120], P('branch'), may hold values from 0.5 to 1.5
- w_qkv: bfloat16 [2, 3, 5120, 3072], P('branch', None, 'seq', 'fsdp'), may hold values from -0.5 to 0.5
- w_out: bfloat16 [2, 3072, 5120], P('branch', 'fsdp', 'seq'), may hold values from -0.109375 to 0.109375
Outputs:
- dmd_grad: float32 [3072, 5120], P('seq', ('branch', 'fsdp'))
- critic_residual: float32 [3072, 5120], P('seq', ('branch', 'fsdp'))
The draws below stay inside these ranges and needn't reach their ends.
All inputs are finite; a program needn't handle non-finite values.
Results may differ from the reference program's by a relative error of at most 0.013.
Values may be sent and summed in bfloat16 or wider, within the bound.
A program may use at most 128 MiB of HBM per device.

```python
import jax
import jax.numpy as jnp
from jax import lax

D = 5120
HEADS = 24
HD = 128
NCOND = 16
L = 3072
N_FSDP = 8


def draw_w_qkv(key, part):
    key_base = jax.random.fold_in(jax.random.fold_in(key, 11), 0)
    shape = (2, 3, D, HEADS * HD)
    stacked = jax.random.normal(key_base, shape, jnp.float32)
    return jnp.clip(stacked * D ** (-0.5), -0.5, 0.5).astype(jnp.bfloat16)


def levels(key, dims, pieces, least, largest):
    def one(axis_at, parts):
        steps = jax.random.uniform(jax.random.fold_in(jax.random.fold_in(key, 6), axis_at), (parts,), jnp.float32, least / len(pieces), largest / len(pieces))
        return jnp.repeat(jnp.exp(steps), dims[axis_at] // parts).reshape((-1,) + (1,) * (len(dims) - axis_at - 1))

    factor_of = one(*pieces[0])
    for cut in pieces[1:]:
        factor_of = factor_of * one(*cut)
    return factor_of


def normal_values(rng, shape, width, limit, pieces=(), held_as=jnp.bfloat16):
    array = jax.random.normal(rng, shape, jnp.float32) * width
    if len(pieces) > 0:
        array = levels(rng, shape, pieces, -0.22, 0.18) * array
    return jnp.clip(array, min=-limit, max=limit).astype(held_as)


def setup_inputs(seed: int = 0) -> dict:
    arg_keys = jax.random.split(jax.random.key(seed), 9)
    return {
        "latents": normal_values(arg_keys[0], (L, D), 1.0, 6.0, ((0, 16),)),
        "noise": normal_values(arg_keys[1], (2, L, D), 1.0, 6.0, ((1, 16),)),
        "time_index": jax.random.randint(arg_keys[2], (2,), 20, 980).astype(jnp.int32),
        "cfg_pair": jax.random.randint(arg_keys[3], (2,), 0, NCOND).astype(jnp.int32),
        "cond_table": normal_values(arg_keys[4], (NCOND, D), 1.0, 6.0, (), jnp.float32),
        "gain": jnp.clip(1.0 + 0.1 * jax.random.normal(arg_keys[5], (2, D), jnp.float32), 0.5, 1.5),
        "w_qkv": draw_w_qkv(jax.random.fold_in(arg_keys[8], 71), 0),
        "w_out": normal_values(arg_keys[7], (2, HEADS * HD, D), (HEADS * HD) ** -0.5, 0.109375, ((0, 2), (1, 8), (2, 16))),
    }


GUIDANCE = 3.5
EPSILON = 1e-06

def sigma_of(step_index):
    fraction = step_index.astype(jnp.float32) / 1000.0
    return 5.0 * fraction / (1.0 + 4.0 * fraction)

def noisy_mix(tokens, noise_rows, step_index):
    noise_level = sigma_of(step_index)
    return (1.0 - noise_level) * tokens + noise_level * noise_rows.astype(jnp.float32)

def normed(noisy_rows, gain_row, shift_row):
    mean_square = lax.optimization_barrier(jnp.mean(noisy_rows * noisy_rows, axis=-1, keepdims=True))
    return (noisy_rows * lax.rsqrt(mean_square + EPSILON) * gain_row + shift_row).astype(jnp.bfloat16)

def head_out(operands):
    query_rows, key_rows, value_rows = operands
    scores = jnp.dot(query_rows, key_rows.T, preferred_element_type=jnp.float32) * HD ** (-0.5)
    peak_score = lax.optimization_barrier(jnp.max(scores, axis=1, keepdims=True))
    softmax_w = jnp.exp(scores - peak_score)
    mass_total = lax.optimization_barrier(jnp.sum(softmax_w, axis=1, keepdims=True))
    mixed = jnp.dot(softmax_w.astype(jnp.bfloat16), value_rows, preferred_element_type=jnp.float32)
    return (mixed / mass_total).astype(jnp.bfloat16)

def section(inputs, weights, out_weight):
    seq_len = inputs.shape[0]
    projected = [jnp.dot(inputs, weights[j], preferred_element_type=jnp.float32).astype(jnp.bfloat16) for j in range(3)]
    per_head = [item.reshape(seq_len, HEADS, HD).transpose(1, 0, 2) for item in projected]
    outputs = lax.map(head_out, (per_head[0], per_head[1], per_head[2]))
    attn = outputs.transpose(1, 0, 2).reshape(seq_len, HEADS * HD)
    col_width = HEADS * HD // N_FSDP
    summed = jnp.zeros((seq_len, out_weight.shape[1]), jnp.float32)
    for group in range(N_FSDP):
        head_part = jnp.dot(attn[:, group * col_width:(group + 1) * col_width], out_weight[group * col_width:(group + 1) * col_width], preferred_element_type=jnp.float32)
        head_part = lax.optimization_barrier(head_part.astype(jnp.bfloat16)).astype(jnp.float32)
        summed = summed + head_part
    return summed

def reference(latents, noise, time_index, cfg_pair, cond_table, gain, w_qkv, w_out):
    tokens = latents.astype(jnp.float32)
    noisy_main = noisy_mix(tokens, noise[0], time_index[0])
    noisy_own = noisy_mix(tokens, noise[1], time_index[1])
    cond_row = cond_table[cfg_pair[0]]
    null_row = cond_table[cfg_pair[1]]
    teacher_cond = section(normed(noisy_main, gain[0], cond_row), w_qkv[0], w_out[0])
    teacher_null = section(normed(noisy_main, gain[0], null_row), w_qkv[0], w_out[0])
    critic_main = section(normed(noisy_main, gain[1], cond_row), w_qkv[1], w_out[1])
    critic_own = section(normed(noisy_own, gain[1], cond_row), w_qkv[1], w_out[1])
    dmd_grad = critic_main - (teacher_null + GUIDANCE * (teacher_cond - teacher_null))
    critic_residual = critic_own - (noise[1].astype(jnp.float32) - tokens)
    return (dmd_grad, critic_residual)
```

```python
import functools

import jax
import jax.numpy as jnp
from jax import lax
from jax.experimental import pallas as pl
from jax.experimental.pallas import tpu as pltpu
from jax.sharding import Mesh
from jax.sharding import PartitionSpec as P

HD = 128
GUIDANCE = 3.5
EPSILON = 1e-06
MESH = pl.DeviceIdType.MESH
BF16, F32 = jnp.bfloat16, jnp.float32

AXES = ("core", "z", "y_hi", "y_lo", "x")
NZ = 8
TOK = 192
DZ = 640
ROWS = 320
COLS = 384
UNITS = 6
RB = 16


def sigma_of(step_index):
    fraction = step_index.astype(F32) / 1000.0
    return 5.0 * fraction / (1.0 + 4.0 * fraction)


def owner_of(unit):
    return unit + unit // 3


def attend_kernel(
    coef, lat_hbm, noise_hbm, shift, gain, w_hbm, out,
    lat, noi, hb, inv, wbuf, acc, units, ub, ob,
    s_in, s_w, r_w, s_h, r_h, s_ring, r_ring, s_sib, r_sib, s_a, r_a, s_kv, r_kv, s_o, r_o,
):
    core, z, y_hi = lax.axis_index("core"), lax.axis_index("z"), lax.axis_index("y_hi")
    swapped = core != y_hi
    sel = lax.rem(core + y_hi, 2)
    partner = {"core": 1 - core, "y_hi": 1 - y_hi}
    sibling = {"core": 1 - core}

    def at_z(step):
        return lax.rem(z + step + NZ, NZ)

    def remote(src, dst, send, recv, device):
        return pltpu.make_async_remote_copy(
            src_ref=src, dst_ref=dst, send_sem=send, recv_sem=recv, device_id=device, device_id_type=MESH
        )

    loads = [
        pltpu.make_async_copy(lat_hbm, lat, s_in.at[0]),
        pltpu.make_async_copy(noise_hbm.at[0], noi.at[0], s_in.at[1]),
        pltpu.make_async_copy(noise_hbm.at[core], noi.at[1], s_in.at[2]),
    ]
    for load in loads:
        load.start()

    barrier = pltpu.get_barrier_semaphore()
    pl.semaphore_signal(barrier, inc=1, device_id=partner, device_id_type=MESH)
    pl.semaphore_signal(barrier, inc=1, device_id=sibling, device_id_type=MESH)
    for step in range(1, NZ):
        pl.semaphore_signal(barrier, inc=1, device_id={"z": at_z(step)}, device_id_type=MESH)
    pl.semaphore_wait(barrier, NZ + 1)

    my_rows = pl.ds(core * ROWS, ROWS)
    sib_rows = pl.ds((1 - core) * ROWS, ROWS)

    def own_local(j):
        return pltpu.make_async_copy(w_hbm.at[j], wbuf.at[z, j, my_rows], r_w.at[j])

    def own_remote(j):
        return remote(
            w_hbm.at[j], wbuf.at[z, j, pl.ds(y_hi * ROWS, ROWS)], s_w.at[j], r_w.at[j], partner
        )

    @pl.when(swapped)
    def _():
        for j in range(3):
            own_remote(j).start()

    @pl.when(jnp.logical_not(swapped))
    def _():
        for j in range(3):
            own_local(j).start()

    def ring(direction, k, j):
        sign = 1 - 2 * direction
        slot = at_z(-sign * (k - 1))
        if k < 4:
            rows = my_rows
        else:
            rows = pl.ds(core * ROWS + direction * (ROWS // 2), ROWS // 2)
        block = wbuf.at[slot, j, rows]
        return remote(
            block, block, s_ring.at[direction, k - 1, j], r_ring.at[direction, k - 1, j], {"z": at_z(sign)}
        )

    def landing(direction, k, j):
        sign = 1 - 2 * direction
        slot = at_z(-sign * k)
        if k < 4:
            rows = my_rows
        else:
            rows = pl.ds(core * ROWS + direction * (ROWS // 2), ROWS // 2)
        block = wbuf.at[slot, j, rows]
        return remote(
            block, block, s_ring.at[direction, k - 1, j], r_ring.at[direction, k - 1, j], {"z": at_z(sign)}
        )

    def to_sibling(index, slot, j):
        block = wbuf.at[slot, j, my_rows]
        return remote(block, block, s_sib.at[index, j], r_sib.at[index, j], sibling)

    def from_sibling(index, slot, j):
        block = wbuf.at[slot, j, sib_rows]
        return remote(block, block, s_sib.at[index, j], r_sib.at[index, j], sibling)

    def begin_ring():
        for j in range(3):
            own_local(j).wait()
            ring(0, 1, j).start()
            ring(1, 1, j).start()
            to_sibling(0, z, j).start()

    pl.when(jnp.logical_not(swapped))(begin_ring)

    for load in loads:
        load.wait()

    def mixed(p, rows, cols):
        return coef[p, 0] * lat[rows, cols].astype(F32) + coef[p, 1] * noi[p, rows, cols].astype(F32)

    for p in range(2):

        @pl.loop(0, TOK // RB)
        def _(b, p=p):
            rows = pl.ds(pl.multiple_of(b * RB, RB), RB)
            total = jnp.zeros((RB, DZ), F32)
            for q in range(NZ):
                part = mixed(p, rows, pl.ds(q * DZ, DZ))
                total = total + part * part
            mean = jnp.sum(total, axis=1, keepdims=True) * (1.0 / (NZ * DZ))
            inv[p, rows, :] = lax.rsqrt(mean + EPSILON)

    def h_copy(slot):
        return remote(hb.at[0, slot], hb.at[1, slot], s_h.at[slot], r_h.at[slot], partner)

    def distance(i):
        return lax.rem(i + 1, 2) * (-((i + 1) // 2)) + lax.rem(i, 2) * ((i + 1) // 2)

    @pl.loop(0, NZ)
    def _(i):
        slot = at_z(distance(i))
        cols = pl.ds(pl.multiple_of(slot * DZ, 128), DZ)
        for p in range(2):

            @pl.loop(0, TOK // RB)
            def _(b, p=p):
                start = pl.multiple_of(b * RB, RB)
                rows = pl.ds(start, RB)
                part = mixed(p, rows, cols) * inv[p, rows, :] * gain[:, cols] + shift[p : p + 1, cols]
                hb[0, slot, pl.ds(p * TOK + start, RB), :] = part.astype(BF16)

        @pl.when(swapped)
        def _():
            h_copy(slot).start()

    pl.when(swapped)(begin_ring)

    acc[...] = jnp.zeros_like(acc)

    def multiply(index, slot):
        for j in range(3):
            from_sibling(index, slot, j).wait_recv()

        @pl.when(swapped)
        def _():
            h_copy(slot).wait_recv()

        @pl.loop(0, 3)
        def _(j):
            acc[j] += jnp.dot(hb[sel, slot], wbuf[slot, j], preferred_element_type=F32)

    groups = [[(0, 0)], [(1, -1), (2, 1)], [(3, -2), (4, 2)], [(5, -3), (6, 3)], [(7, 4)]]
    for k in range(1, 5):
        for j in range(3):
            for direction in range(2):
                landing(direction, k, j).wait_recv()
                if k < 4:
                    ring(direction, k + 1, j).start()
                    index, step = groups[k][direction]
                    to_sibling(index, at_z(step), j).start()
            if k == 4:
                index, step = groups[k][0]
                to_sibling(index, at_z(step), j).start()
        for index, step in groups[k - 1]:
            multiply(index, at_z(step))
    for index, step in groups[4]:
        multiply(index, at_z(step))

    my_part = pl.ds(z * TOK, TOK)

    def unit_remote(u):
        return remote(
            units.at[u], ub.at[:, core, my_part], s_a.at[u], r_a.at[z], {"z": owner_of(u)}
        )

    def unit_local(u):
        return pltpu.make_async_copy(units.at[u], ub.at[:, core, my_part], r_a.at[z])

    for u in range(UNITS):
        p, h = u // 3, u % 3
        for j in range(3):
            units[u, j] = acc[j, p * TOK : (p + 1) * TOK, h * HD : (h + 1) * HD].astype(BF16)

        @pl.when(z == owner_of(u))
        def _(u=u):
            unit_local(u).start()

        @pl.when(z != owner_of(u))
        def _(u=u):
            unit_remote(u).start()

    is_owner = lax.rem(z, 4) != 3
    mine = jnp.minimum(z - z // 4, UNITS - 1)

    def arrived(source):
        block = ub.at[:, core, pl.ds(source * TOK, TOK)]
        return remote(block, block, s_a.at[0], r_a.at[source], sibling)

    def kv_to_sibling(source, which):
        block = ub.at[pl.ds(1, 2), which, pl.ds(source * TOK, TOK)]
        return remote(block, block, s_kv.at[source], r_kv.at[source], sibling)

    def o_remote(to):
        return remote(ob.at[to], out.at[mine], s_o.at[to], r_o.at[mine], {"z": to})

    def o_local(to):
        return pltpu.make_async_copy(ob.at[to], out.at[mine], r_o.at[mine])

    @pl.when(is_owner)
    def _():
        @pl.loop(0, NZ)
        def _(i):
            source = at_z(distance(i))
            arrived(source).wait_recv()
            kv_to_sibling(source, core).start()

        @pl.loop(0, NZ)
        def _(i):
            kv_to_sibling(at_z(distance(i)), 1 - core).wait_recv()

        @pl.loop(0, NZ)
        def _(i):
            to = at_z(distance(NZ - 1 - i))
            queries = ub[0, core, pl.ds(pl.multiple_of(to * TOK, TOK), TOK), :]
            keys = ub[1].reshape(2 * NZ * TOK, HD)
            scores = lax.dot_general(
                queries, keys, (((1,), (1,)), ((), ())), preferred_element_type=F32
            ) * (HD**-0.5)
            peak = jnp.max(scores, axis=1, keepdims=True)
            weight = jnp.exp(scores - peak)
            mass = jnp.sum(weight, axis=1, keepdims=True)
            result = jnp.dot(
                weight.astype(BF16), ub[2].reshape(2 * NZ * TOK, HD), preferred_element_type=F32
            )
            ob[to] = (result / mass).astype(BF16)

            @pl.when(to == z)
            def _():
                o_local(to).start()

            @pl.when(to != z)
            def _():
                o_remote(to).start()

    for u in range(UNITS):
        block = out.at[u]
        remote(block, block, s_o.at[0], r_o.at[u], sibling).wait_recv()

    @pl.when(swapped)
    def _():
        for j in range(3):
            own_remote(j).wait_send()
        for slot in range(NZ):
            h_copy(slot).wait_send()

    for k in range(1, 5):
        for j in range(3):
            for direction in range(2):
                ring(direction, k, j).wait_send()
    for group in groups:
        for index, step in group:
            for j in range(3):
                to_sibling(index, at_z(step), j).wait_send()
    for u in range(UNITS):

        @pl.when(z != owner_of(u))
        def _(u=u):
            unit_remote(u).wait_send()

    @pl.when(is_owner)
    def _():
        for source in range(NZ):
            kv_to_sibling(source, core).wait_send()

            @pl.when(z != source)
            def _(source=source):
                o_remote(source).wait_send()


def attend(coef, latents, noise, shift, gain, w_qkv):
    dma = pltpu.SemaphoreType.DMA
    vmem, any_space = pl.BlockSpec(memory_space=pltpu.VMEM), pl.BlockSpec(memory_space=pl.ANY)
    return pl.pallas_call(
        attend_kernel,
        out_shape=jax.ShapeDtypeStruct((UNITS, TOK, HD), BF16),
        in_specs=[pl.BlockSpec(memory_space=pltpu.SMEM), any_space, any_space, vmem, vmem, any_space],
        out_specs=vmem,
        scratch_shapes=[
            pltpu.VMEM((TOK, NZ * DZ), BF16),
            pltpu.VMEM((2, TOK, NZ * DZ), BF16),
            pltpu.VMEM((2, NZ, 2 * TOK, DZ), BF16),
            pltpu.VMEM((2, TOK, 1), F32),
            pltpu.VMEM((NZ, 3, DZ, COLS), BF16),
            pltpu.VMEM((3, 2 * TOK, COLS), F32),
            pltpu.VMEM((UNITS, 3, TOK, HD), BF16),
            pltpu.VMEM((3, 2, NZ * TOK, HD), BF16),
            pltpu.VMEM((NZ, TOK, HD), BF16),
            dma((3,)),
            dma((3,)), dma((3,)),
            dma((NZ,)), dma((NZ,)),
            dma((2, 4, 3)), dma((2, 4, 3)),
            dma((NZ, 3)), dma((NZ, 3)),
            dma((UNITS,)), dma((NZ,)),
            dma((NZ,)), dma((NZ,)),
            dma((NZ,)), dma((UNITS,)),
        ],
        compiler_params=pltpu.CompilerParams(
            collective_id=0, has_side_effects=True, vmem_limit_bytes=58 * 2**20
        ),
        cost_estimate=pl.CostEstimate(
            flops=9_000_000_000, bytes_accessed=40_000_000, transcendentals=5_000_000
        ),
    )(coef, latents, noise, shift, gain, w_qkv)


def body(latents, noise, time_index, cfg_pair, cond_table, gain, w_qkv, w_out):
    core = lax.axis_index("core")
    levels = sigma_of(time_index)
    level = jnp.stack([levels[0], levels[core]])
    coef = jnp.stack([1.0 - level, level], axis=1)
    second = cfg_pair[1 - core]
    shift = jnp.concatenate(
        [
            lax.dynamic_slice_in_dim(cond_table, cfg_pair[0], 1, 0),
            lax.dynamic_slice_in_dim(cond_table, second, 1, 0),
        ]
    )
    attn = attend(coef, latents, noise, shift, gain, w_qkv[0])
    attn = attn.reshape(2, 3, TOK, HD).transpose(0, 2, 1, 3).reshape(2, TOK, COLS)

    across = ("core", "y_hi")
    w_own = lax.ppermute(w_out[0], across, [(0, 0), (1, 2), (2, 1), (3, 3)])
    out_full = lax.all_gather(lax.all_gather(w_own, "core", axis=1, tiled=True), "z", axis=1, tiled=True)
    partial_value = jnp.einsum("ptc,cd->ptd", attn, out_full, preferred_element_type=F32).astype(BF16)
    blocks = partial_value.reshape(2, TOK, 2, 8, ROWS).transpose(3, 2, 0, 1, 4)
    blocks = lax.all_to_all(blocks, ("y_lo", "x"), 0, 0, tiled=True)
    sums = jnp.sum(blocks.astype(F32), axis=0).astype(BF16)
    y_hi = lax.axis_index("y_hi")
    own = lax.ppermute(sums[y_hi], across, [(0, 0), (1, 2), (2, 1), (3, 3)]).astype(F32)
    other = lax.ppermute(sums[1 - y_hi], across, [(0, 2), (1, 0), (2, 3), (3, 1)]).astype(F32)
    is_teacher = core == 0
    teacher = jnp.where(is_teacher, own, other)
    critic = jnp.where(is_teacher, other, own)
    dmd_grad = critic[0] - (teacher[1] + GUIDANCE * (teacher[0] - teacher[1]))
    col_start = (core * 8 + lax.axis_index("y_lo") * 4 + lax.axis_index("x")) * ROWS
    noise_cols = lax.dynamic_slice_in_dim(noise[1], col_start, ROWS, 1).astype(F32)
    latent_cols = lax.dynamic_slice_in_dim(latents, col_start, ROWS, 1).astype(F32)
    return dmd_grad, critic[1] - (noise_cols - latent_cols)


def solution(mesh):
    torus = Mesh(mesh.devices.reshape(2, NZ, 2, 2, 4), AXES)
    seq, fsdp = ("z", "y_hi"), ("y_lo", "x")
    return jax.shard_map(
        body,
        mesh=torus,
        in_specs=(
            P(seq, None),
            P(None, seq, None),
            P(),
            P(),
            P(),
            P("core", None),
            P("core", None, seq, fsdp),
            P("core", fsdp, seq),
        ),
        out_specs=(P(seq, ("core", *fsdp)), P(seq, ("core", *fsdp))),
        check_vma=False,
    )
```

```python
import functools

import jax
import jax.numpy as jnp
from jax import lax
from jax.experimental import pallas as pl
from jax.experimental.pallas import tpu as pltpu
from jax.sharding import Mesh
from jax.sharding import PartitionSpec as P

HD = 128
LOG2E = 1.4426950408889634
GUIDANCE = 3.5
EPSILON = 1e-06
MESH = pl.DeviceIdType.MESH
BF16, F32 = jnp.bfloat16, jnp.float32

AXES = ("core", "z", "y_hi", "y_lo", "x")
NZ = 8
TOK = 192
DZ = 640
ROWS = 320
COLS = 384
UNITS = 6
RB = 64


def owner_of(unit):
    return unit + unit // 3


def step_kernel(
    times, pair, lat_hbm, noise_hbm, cond, gain, w_hbm, wo_hbm, fin,
    lat, noi, shift, hb, inv, wbuf, acc, units, ub, ob, att, wo, pred, pb,
    s_in, s_w, r_w, s_h, r_h, s_ring, r_ring, s_sib, r_sib, s_a, r_a, s_kv, r_kv, s_o, r_o,
    s_wa, s_wo, r_wo, s_att, r_att, s_f, r_f,
):
    core, z, y_hi = lax.axis_index("core"), lax.axis_index("z"), lax.axis_index("y_hi")
    y_lo, x = lax.axis_index("y_lo"), lax.axis_index("x")
    f = y_lo * 4 + x
    swapped = core != y_hi
    sel = lax.rem(core + y_hi, 2)
    partner = {"core": 1 - core, "y_hi": 1 - y_hi}
    sibling = {"core": 1 - core}

    def at_z(step):
        return lax.rem(z + step + NZ, NZ)

    def at_f(step):
        return lax.rem(f + step, 8)

    def f_device(peer):
        return {"y_lo": peer // 4, "x": lax.rem(peer, 4)}

    def remote(src, dst, send, recv, device):
        return pltpu.make_async_remote_copy(
            src_ref=src, dst_ref=dst, send_sem=send, recv_sem=recv, device_id=device, device_id_type=MESH
        )

    loads = [
        pltpu.make_async_copy(lat_hbm, lat, s_in.at[0]),
        pltpu.make_async_copy(noise_hbm.at[0], noi.at[0], s_in.at[1]),
        pltpu.make_async_copy(noise_hbm.at[core], noi.at[1], s_in.at[2]),
    ]
    for load in loads:
        load.start()

    half_in = z // 4
    in_y_lo, in_x = lax.rem(z, 4) // 2, 2 * lax.rem(z, 2) + y_hi
    in_place = (y_lo == core) & (y_hi == core) & (in_y_lo == y_lo) & (in_x == x)
    takes_in = (lax.rem(z, 4) // 2 == y_lo) & (lax.rem(z, 2) == x // 2)

    barrier = pltpu.get_barrier_semaphore()

    def greet(device):
        pl.semaphore_signal(barrier, inc=1, device_id=device, device_id_type=MESH)

    greet(partner)
    greet(sibling)
    greet({"y_hi": 1 - y_hi})
    for step in range(1, NZ):
        greet({"z": at_z(step)})
    for step in range(1, 8):
        greet(f_device(at_f(step)))
    for source_x in range(4):
        from_self = (y_hi == core) & (lax.rem(x, 2) == y_hi) & (y_lo == core) & (x == source_x)

        @pl.when(takes_in & jnp.logical_not(from_self))
        def _(source_x=source_x):
            greet({"core": y_hi, "y_hi": lax.rem(x, 2), "y_lo": core, "x": source_x})

    @pl.when(in_place)
    def _():
        pl.semaphore_wait(barrier, 17)

    @pl.when(jnp.logical_not(in_place))
    def _():
        pl.semaphore_wait(barrier, 18)

    my_rows = pl.ds(core * ROWS, ROWS)
    sib_rows = pl.ds((1 - core) * ROWS, ROWS)

    def own_local(j):
        return pltpu.make_async_copy(w_hbm.at[0, j], wbuf.at[z, j, my_rows], r_w.at[j])

    def own_remote(j):
        return remote(
            w_hbm.at[0, j], wbuf.at[z, j, pl.ds(y_hi * ROWS, ROWS)], s_w.at[j], r_w.at[j], partner
        )

    @pl.when(swapped)
    def _():
        for j in range(3):
            own_remote(j).start()

    @pl.when(jnp.logical_not(swapped))
    def _():
        for j in range(3):
            own_local(j).start()

    def ring_copy(direction, k, j, moved):
        sign = 1 - 2 * direction
        slot = at_z(-sign * (k - 1 + moved))
        if k < 4:
            rows = my_rows
        else:
            rows = pl.ds(core * ROWS + direction * (ROWS // 2), ROWS // 2)
        block = wbuf.at[slot, j, rows]
        return remote(
            block, block, s_ring.at[direction, k - 1, j], r_ring.at[direction, k - 1, j], {"z": at_z(sign)}
        )

    def ring(direction, k, j):
        return ring_copy(direction, k, j, 0)

    def landing(direction, k, j):
        return ring_copy(direction, k, j, 1)

    def to_sibling(index, slot, j):
        block = wbuf.at[slot, j, my_rows]
        return remote(block, block, s_sib.at[index, j], r_sib.at[index, j], sibling)

    def from_sibling(index, slot, j):
        block = wbuf.at[slot, j, sib_rows]
        return remote(block, block, s_sib.at[index, j], r_sib.at[index, j], sibling)

    def begin_ring():
        for j in range(3):
            own_local(j).wait()
            ring(0, 1, j).start()
            ring(1, 1, j).start()
            to_sibling(0, z, j).start()

    pl.when(jnp.logical_not(swapped))(begin_ring)

    def wo_in():
        return remote(
            wo_hbm, wo.at[half_in, f], s_wa.at[0], r_wo.at[half_in, f],
            {"core": y_lo, "y_hi": core, "y_lo": in_y_lo, "x": in_x},
        )

    @pl.when(in_place)
    def _():
        pltpu.make_async_copy(wo_hbm, wo.at[half_in, f], r_wo.at[half_in, f]).start()

    @pl.when(jnp.logical_not(in_place))
    def _():
        wo_in().start()

    def level_of(step_index):
        fraction = jnp.full((8, 128), step_index.astype(F32)) / 1000.0
        return (5.0 * fraction / (1.0 + 4.0 * fraction))[0:1, 0:1]

    levels = (level_of(times[0]), level_of(times[core]))
    shift[0:1, :] = cond[pl.ds(pair[0], 1), :]
    shift[1:2, :] = cond[pl.ds(pair[1 - core], 1), :]
    for load in loads:
        load.wait()

    def mixed(p, rows, cols):
        return (1.0 - levels[p]) * lat[rows, cols].astype(F32) + levels[p] * noi[p, rows, cols].astype(F32)

    for p in range(2):

        @pl.loop(0, TOK // 16)
        def _(b, p=p):
            rows = pl.ds(pl.multiple_of(b * 16, 16), 16)
            total = jnp.zeros((16, DZ), F32)
            for q in range(NZ):
                part = mixed(p, rows, pl.ds(q * DZ, DZ))
                total = total + part * part
            mean = jnp.sum(total, axis=1, keepdims=True) * (1.0 / (NZ * DZ))
            inv[p, rows, :] = lax.rsqrt(mean + EPSILON)

    pl.when(swapped)(begin_ring)

    def h_copy(slot):
        return remote(hb.at[0, slot], hb.at[1, slot], s_h.at[slot], r_h.at[slot], partner)

    def distance(i):
        return lax.rem(i + 1, 2) * (-((i + 1) // 2)) + lax.rem(i, 2) * ((i + 1) // 2)

    def make_inputs(first, count):
        @pl.loop(first, first + count)
        def _(i):
            slot = at_z(distance(i))
            cols = pl.ds(pl.multiple_of(slot * DZ, 128), DZ)
            for p in range(2):

                @pl.loop(0, TOK // RB)
                def _(b, p=p):
                    start = pl.multiple_of(b * RB, RB)
                    rows = pl.ds(start, RB)
                    part = mixed(p, rows, cols) * inv[p, rows, :] * gain[:, cols] + shift[p : p + 1, cols]
                    hb[0, slot, pl.ds(p * TOK + start, RB), :] = part.astype(BF16)

            @pl.when(swapped)
            def _():
                h_copy(slot).start()

    acc[...] = jnp.zeros_like(acc)

    def multiply(index, slot):
        for j in range(3):
            from_sibling(index, slot, j).wait_recv()

        @pl.when(swapped)
        def _():
            h_copy(slot).wait_recv()

        @pl.loop(0, 3)
        def _(j):
            acc[j] += jnp.dot(hb[sel, slot], wbuf[slot, j], preferred_element_type=F32)

    groups = [[(0, 0)], [(1, -1), (2, 1)], [(3, -2), (4, 2)], [(5, -3), (6, 3)], [(7, 4)]]
    make_inputs(0, 2)
    for k in range(1, 5):
        for j in range(3):
            for direction in range(2):
                landing(direction, k, j).wait_recv()
                if k < 4:
                    ring(direction, k + 1, j).start()
                    index, step = groups[k][direction]
                    to_sibling(index, at_z(step), j).start()
            if k == 4:
                index, step = groups[k][0]
                to_sibling(index, at_z(step), j).start()
            if k == 1:
                make_inputs(2 + 2 * j, 2)
        for index, step in groups[k - 1]:
            multiply(index, at_z(step))
    for index, step in groups[4]:
        multiply(index, at_z(step))

    my_part = pl.ds(z * TOK, TOK)

    def unit_remote(u):
        return remote(
            units.at[u], ub.at[:, core, my_part], s_a.at[u], r_a.at[z], {"z": owner_of(u)}
        )

    def unit_local(u):
        return pltpu.make_async_copy(units.at[u], ub.at[:, core, my_part], r_a.at[z])

    for u in range(UNITS):
        p, h = u // 3, u % 3
        for j in range(3):
            units[u, j] = acc[j, p * TOK : (p + 1) * TOK, h * HD : (h + 1) * HD].astype(BF16)

        @pl.when(z == owner_of(u))
        def _(u=u):
            unit_local(u).start()

        @pl.when(z != owner_of(u))
        def _(u=u):
            unit_remote(u).start()

    def wo_tick(t, act):
        for half in range(2):
            delta = lax.rem(z - (half * 4 + y_lo * 2 + x // 2) + NZ, NZ)
            b = t - (jnp.minimum(delta, NZ - delta) + 1)

            @pl.when((b >= 0) & (b < 4))
            def _(half=half, delta=delta, b=b):
                slot = core * 4 + b
                block = wo.at[half, slot]

                def copy(lane, device):
                    return remote(block, block, s_wo.at[lane, half, slot], r_wo.at[half, slot], device)

                if act == "send":
                    copy(2, sibling).wait_recv()
                right = (delta <= 2) | ((delta == 3) & (b < 2))
                left = (delta == 0) | (delta >= 6) | ((delta == 5) & (b >= 2))
                for lane, go, device in ((0, right, {"z": at_z(1)}), (1, left, {"z": at_z(-1)})):

                    @pl.when(go)
                    def _(lane=lane, device=device):
                        if act == "send":
                            copy(lane, device).start()
                        else:
                            copy(lane, device).wait_send()

                if act == "send":
                    copy(2, sibling).start()
                else:
                    copy(2, sibling).wait_send()

    is_owner = lax.rem(z, 4) != 3
    mine = jnp.minimum(z - z // 4, UNITS - 1)
    mine_rows = pl.ds(pl.multiple_of((mine // 3) * TOK, TOK), TOK)
    mine_cols = pl.ds(pl.multiple_of(lax.rem(mine, 3) * HD, HD), HD)

    def arrived(source):
        block = ub.at[:, core, pl.ds(source * TOK, TOK)]
        return remote(block, block, s_a.at[0], r_a.at[source], sibling)

    def kv_to_sibling(source, which):
        block = ub.at[pl.ds(1, 2), which, pl.ds(source * TOK, TOK)]
        return remote(block, block, s_kv.at[source], r_kv.at[source], sibling)

    def o_remote(to):
        return remote(ob.at[to], att.at[f, mine_rows, mine_cols], s_o.at[to], r_o.at[mine], {"z": to})

    def o_local(to):
        return pltpu.make_async_copy(ob.at[to], att.at[f, mine_rows, mine_cols], r_o.at[mine])

    @pl.when(is_owner)
    def _():
        @pl.loop(0, NZ)
        def _(i):
            source = at_z(distance(i))
            arrived(source).wait_recv()
            kv_to_sibling(source, core).start()

        @pl.loop(0, NZ)
        def _(i):
            kv_to_sibling(at_z(distance(i)), 1 - core).wait_recv()

    wo_tick(1, "send")

    @pl.loop(0, NZ)
    def _(i):
        to = at_z(distance(NZ - 1 - i))

        @pl.when(is_owner)
        def _():
            queries = ub[0, core, pl.ds(pl.multiple_of(to * TOK, TOK), TOK), :]
            keys = ub[1].reshape(2 * NZ * TOK, HD)
            scores = lax.dot_general(
                queries, keys, (((1,), (1,)), ((), ())), preferred_element_type=F32
            )
            peak = jnp.max(scores, axis=1, keepdims=True)
            weight = jnp.exp2((scores - peak) * (HD**-0.5 * LOG2E))
            mass = jnp.sum(weight, axis=1, keepdims=True)
            result = jnp.dot(
                weight.astype(BF16), ub[2].reshape(2 * NZ * TOK, HD), preferred_element_type=F32
            )
            ob[to] = (result / mass).astype(BF16)

            @pl.when(to == z)
            def _():
                o_local(to).start()

            @pl.when(to != z)
            def _():
                o_remote(to).start()

        @pl.when(lax.rem(i, 3) == 2)
        def _():
            wo_tick(2 + i // 3, "send")

    wo_tick(4, "send")

    def att_copy(source, p, peer):
        block = att.at[source, pl.ds(p * TOK, TOK)]
        return remote(block, block, s_att.at[peer, p], r_att.at[source, p], f_device(peer))

    for p in range(2):
        for h in range(3):
            block = att.at[f, pl.ds(p * TOK, TOK), pl.ds(h * HD, HD)]
            remote(block, block, s_o.at[0], r_o.at[p * 3 + h], sibling).wait_recv()
        for step in (1, 7, 4, 3, 5, 2, 6):
            att_copy(f, p, at_f(step)).start()
        wo_tick(5 + p, "send")
    wo_tick(7, "send")
    wo_tick(8, "send")

    pred[...] = jnp.zeros_like(pred)

    @pl.loop(0, 8)
    def _(step):
        source = at_f(step)

        @pl.when(step > 0)
        def _():
            for p in range(2):
                att_copy(source, p, source).wait_recv()

        for half in range(2):

            @pl.when(source // 4 != core)
            def _(half=half):
                block = wo.at[half, source]
                remote(block, block, s_wo.at[2, half, source], r_wo.at[half, source], sibling).wait_recv()

            pred[half] += lax.dot_general(
                att[source], wo[half, source], (((1,), (1,)), ((), ())), preferred_element_type=F32
            )

    def fin_copy(half):
        return remote(
            pb.at[half], fin.at[y_hi], s_f.at[half], r_f.at[y_hi], {"core": half, "y_hi": core}
        )

    for half in range(2):
        stays = (core == half) & (y_hi == core)
        pb[half] = pred[half].astype(BF16)

        @pl.when(stays)
        def _(half=half):
            pltpu.make_async_copy(pb.at[half], fin.at[y_hi], r_f.at[y_hi]).start()

        @pl.when(jnp.logical_not(stays))
        def _(half=half):
            fin_copy(half).start()

    for section in range(2):
        block = fin.at[section]
        remote(block, block, s_f.at[0], r_f.at[section], sibling).wait_recv()

    @pl.when(swapped)
    def _():
        for j in range(3):
            own_remote(j).wait_send()
        for slot in range(NZ):
            h_copy(slot).wait_send()

    @pl.when(jnp.logical_not(in_place))
    def _():
        wo_in().wait_send()

    for k in range(1, 5):
        for j in range(3):
            for direction in range(2):
                ring(direction, k, j).wait_send()
    for group in groups:
        for index, step in group:
            for j in range(3):
                to_sibling(index, at_z(step), j).wait_send()
    for u in range(UNITS):

        @pl.when(z != owner_of(u))
        def _(u=u):
            unit_remote(u).wait_send()

    @pl.when(is_owner)
    def _():
        for source in range(NZ):
            kv_to_sibling(source, core).wait_send()

            @pl.when(z != source)
            def _(source=source):
                o_remote(source).wait_send()

    @pl.loop(1, 9)
    def _(t):
        wo_tick(t, "wait")

    for p in range(2):
        for step in range(1, 8):
            att_copy(f, p, at_f(step)).wait_send()
    for half in range(2):

        @pl.when(jnp.logical_not((core == half) & (y_hi == core)))
        def _(half=half):
            fin_copy(half).wait_send()


def predictions(times, pair, latents, noise, cond_table, gain, w_qkv, w_out):
    dma = pltpu.SemaphoreType.DMA
    vmem, any_space = pl.BlockSpec(memory_space=pltpu.VMEM), pl.BlockSpec(memory_space=pl.ANY)
    smem = pl.BlockSpec(memory_space=pltpu.SMEM)
    return pl.pallas_call(
        step_kernel,
        out_shape=jax.ShapeDtypeStruct((2, 2 * TOK, ROWS), BF16),
        in_specs=[smem, smem, any_space, any_space, vmem, vmem, any_space, any_space],
        out_specs=vmem,
        scratch_shapes=[
            pltpu.VMEM((TOK, NZ * DZ), BF16),
            pltpu.VMEM((2, TOK, NZ * DZ), BF16),
            pltpu.VMEM((2, NZ * DZ), F32),
            pltpu.VMEM((2, NZ, 2 * TOK, DZ), BF16),
            pltpu.VMEM((2, TOK, 1), F32),
            pltpu.VMEM((NZ, 3, DZ, COLS), BF16),
            pltpu.VMEM((3, 2 * TOK, COLS), F32),
            pltpu.VMEM((UNITS, 3, TOK, HD), BF16),
            pltpu.VMEM((3, 2, NZ * TOK, HD), BF16),
            pltpu.VMEM((NZ, TOK, HD), BF16),
            pltpu.VMEM((8, 2 * TOK, COLS), BF16),
            pltpu.VMEM((2, 8, ROWS, COLS), BF16),
            pltpu.VMEM((2, 2 * TOK, ROWS), F32),
            pltpu.VMEM((2, 2 * TOK, ROWS), BF16),
            dma((3,)),
            dma((3,)), dma((3,)),
            dma((NZ,)), dma((NZ,)),
            dma((2, 4, 3)), dma((2, 4, 3)),
            dma((NZ, 3)), dma((NZ, 3)),
            dma((UNITS,)), dma((NZ,)),
            dma((NZ,)), dma((NZ,)),
            dma((NZ,)), dma((UNITS,)),
            dma((1,)), dma((3, 2, 8)), dma((2, 8)),
            dma((8, 2)), dma((8, 2)),
            dma((2,)), dma((2,)),
        ],
        compiler_params=pltpu.CompilerParams(
            collective_id=0, has_side_effects=True, vmem_limit_bytes=60 * 2**20
        ),
        cost_estimate=pl.CostEstimate(
            flops=9_000_000_000, bytes_accessed=40_000_000, transcendentals=5_000_000
        ),
    )(times, pair, latents, noise, cond_table, gain, w_qkv, w_out)


def body(latents, noise, time_index, cfg_pair, cond_table, gain, w_qkv, w_out):
    found = predictions(
        time_index, cfg_pair, latents, noise, cond_table, gain, w_qkv, jnp.swapaxes(w_out[0], 0, 1)
    )
    sums = found.reshape(2, 2, TOK, ROWS).astype(F32)
    teacher, critic = sums[0], sums[1]
    dmd_grad = critic[0] - (teacher[1] + GUIDANCE * (teacher[0] - teacher[1]))
    col_start = (lax.axis_index("core") * 8 + lax.axis_index("y_lo") * 4 + lax.axis_index("x")) * ROWS
    noise_cols = lax.dynamic_slice_in_dim(noise[1], col_start, ROWS, 1).astype(F32)
    latent_cols = lax.dynamic_slice_in_dim(latents, col_start, ROWS, 1).astype(F32)
    return dmd_grad, critic[1] - (noise_cols - latent_cols)


def solution(mesh):
    torus = Mesh(mesh.devices.reshape(2, NZ, 2, 2, 4), AXES)
    seq, fsdp = ("z", "y_hi"), ("y_lo", "x")
    return jax.shard_map(
        body,
        mesh=torus,
        in_specs=(
            P(seq, None),
            P(None, seq, None),
            P(),
            P(),
            P(),
            P("core", None),
            P("core", None, seq, fsdp),
            P("core", fsdp, seq),
        ),
        out_specs=(P(seq, ("core", *fsdp)), P(seq, ("core", *fsdp))),
        check_vma=False,
    )
```

```python
import functools

import jax
import jax.numpy as jnp
from jax import lax
from jax.experimental import pallas as pl
from jax.experimental.pallas import tpu as pltpu
from jax.sharding import Mesh
from jax.sharding import PartitionSpec as P

HD = 128
LOG2E = 1.4426950408889634
GUIDANCE = 3.5
EPSILON = 1e-06
MESH = pl.DeviceIdType.MESH
BF16, F32 = jnp.bfloat16, jnp.float32

AXES = ("core", "z", "y_hi", "y_lo", "x")
NZ = 8
TOK = 192
DZ = 640
ROWS = 320
COLS = 384
UNITS = 6
RB = 64


def owner_of(unit):
    return unit + unit // 3


def step_kernel(
    times, pair, lat_hbm, noise_hbm, cond, gain, w_hbm, wo_hbm, dmd, residual,
    lat, noi, shift, hb, inv, wbuf, acc, units, ub, ob, att, wo, pred, pb, fin, target, base,
    s_in, s_w, r_w, s_h, r_h, s_ring, r_ring, s_sib, r_sib, s_a, r_a, s_kv, r_kv, s_o, r_o,
    s_wa, s_wo, r_wo, s_att, r_att, s_f, r_f,
):
    core, z, y_hi = lax.axis_index("core"), lax.axis_index("z"), lax.axis_index("y_hi")
    y_lo, x = lax.axis_index("y_lo"), lax.axis_index("x")
    f = y_lo * 4 + x
    swapped = core != y_hi
    sel = lax.rem(core + y_hi, 2)
    partner = {"core": 1 - core, "y_hi": 1 - y_hi}
    sibling = {"core": 1 - core}

    def at_z(step):
        return lax.rem(z + step + NZ, NZ)

    def at_f(step):
        return lax.rem(f + step, 8)

    def f_device(peer):
        return {"y_lo": peer // 4, "x": lax.rem(peer, 4)}

    def remote(src, dst, send, recv, device):
        return pltpu.make_async_remote_copy(
            src_ref=src, dst_ref=dst, send_sem=send, recv_sem=recv, device_id=device, device_id_type=MESH
        )

    loads = [
        pltpu.make_async_copy(lat_hbm, lat, s_in.at[0]),
        pltpu.make_async_copy(noise_hbm.at[0], noi.at[0], s_in.at[1]),
        pltpu.make_async_copy(noise_hbm.at[core], noi.at[1], s_in.at[2]),
    ]
    out_block = core * 8 + f
    window = pl.ds(pl.multiple_of(((out_block * 5) // 2) * 128, 128), COLS)
    target_load = pltpu.make_async_copy(noise_hbm.at[1, :, window], target, s_in.at[3])
    target_load.start()
    for load in loads:
        load.start()

    half_in = z // 4
    in_y_lo, in_x = lax.rem(z, 4) // 2, 2 * lax.rem(z, 2) + y_hi
    in_place = (y_lo == core) & (y_hi == core) & (in_y_lo == y_lo) & (in_x == x)
    takes_in = (lax.rem(z, 4) // 2 == y_lo) & (lax.rem(z, 2) == x // 2)

    barrier = pltpu.get_barrier_semaphore()

    def greet(device):
        pl.semaphore_signal(barrier, inc=1, device_id=device, device_id_type=MESH)

    greet(partner)
    greet(sibling)
    greet({"y_hi": 1 - y_hi})
    for step in range(1, NZ):
        greet({"z": at_z(step)})
    for step in range(1, 8):
        greet(f_device(at_f(step)))
    for source_x in range(4):
        from_self = (y_hi == core) & (lax.rem(x, 2) == y_hi) & (y_lo == core) & (x == source_x)

        @pl.when(takes_in & jnp.logical_not(from_self))
        def _(source_x=source_x):
            greet({"core": y_hi, "y_hi": lax.rem(x, 2), "y_lo": core, "x": source_x})

    @pl.when(in_place)
    def _():
        pl.semaphore_wait(barrier, 17)

    @pl.when(jnp.logical_not(in_place))
    def _():
        pl.semaphore_wait(barrier, 18)

    my_rows = pl.ds(core * ROWS, ROWS)
    sib_rows = pl.ds((1 - core) * ROWS, ROWS)

    def own_local(j):
        return pltpu.make_async_copy(w_hbm.at[0, j], wbuf.at[z, j, my_rows], r_w.at[j])

    def own_remote(j):
        return remote(
            w_hbm.at[0, j], wbuf.at[z, j, pl.ds(y_hi * ROWS, ROWS)], s_w.at[j], r_w.at[j], partner
        )

    @pl.when(swapped)
    def _():
        for j in range(3):
            own_remote(j).start()

    @pl.when(jnp.logical_not(swapped))
    def _():
        for j in range(3):
            own_local(j).start()

    def ring_copy(direction, k, j, moved):
        sign = 1 - 2 * direction
        slot = at_z(-sign * (k - 1 + moved))
        if k < 4:
            rows = my_rows
        else:
            rows = pl.ds(core * ROWS + direction * (ROWS // 2), ROWS // 2)
        block = wbuf.at[slot, j, rows]
        return remote(
            block, block, s_ring.at[direction, k - 1, j], r_ring.at[direction, k - 1, j], {"z": at_z(sign)}
        )

    def ring(direction, k, j):
        return ring_copy(direction, k, j, 0)

    def landing(direction, k, j):
        return ring_copy(direction, k, j, 1)

    def to_sibling(index, slot, j):
        block = wbuf.at[slot, j, my_rows]
        return remote(block, block, s_sib.at[index, j], r_sib.at[index, j], sibling)

    def from_sibling(index, slot, j):
        block = wbuf.at[slot, j, sib_rows]
        return remote(block, block, s_sib.at[index, j], r_sib.at[index, j], sibling)

    def begin_ring():
        for j in range(3):
            own_local(j).wait()
            ring(0, 1, j).start()
            ring(1, 1, j).start()
            to_sibling(0, z, j).start()

    pl.when(jnp.logical_not(swapped))(begin_ring)

    def wo_part(part):
        return pl.ds(part * (ROWS // 2), ROWS // 2)

    def wo_in(part):
        return remote(
            wo_hbm.at[wo_part(part)], wo.at[half_in, f, wo_part(part)], s_wa.at[part], r_wo.at[half_in, f, part],
            {"core": y_lo, "y_hi": core, "y_lo": in_y_lo, "x": in_x},
        )

    @pl.when(in_place)
    def _():
        for part in range(2):
            pltpu.make_async_copy(
                wo_hbm.at[wo_part(part)], wo.at[half_in, f, wo_part(part)], r_wo.at[half_in, f, part]
            ).start()

    @pl.when(jnp.logical_not(in_place))
    def _():
        for part in range(2):
            wo_in(part).start()

    def level_of(step_index):
        fraction = jnp.full((8, 128), step_index.astype(F32)) / 1000.0
        return (5.0 * fraction / (1.0 + 4.0 * fraction))[0:1, 0:1]

    levels = (level_of(times[0]), level_of(times[core]))
    shift[0:1, :] = cond[pl.ds(pair[0], 1), :]
    shift[1:2, :] = cond[pl.ds(pair[1 - core], 1), :]
    for load in loads:
        load.wait()

    def mixed(p, rows, cols):
        return (1.0 - levels[p]) * lat[rows, cols].astype(F32) + levels[p] * noi[p, rows, cols].astype(F32)

    for p in range(2):

        @pl.loop(0, TOK // 16)
        def _(b, p=p):
            rows = pl.ds(pl.multiple_of(b * 16, 16), 16)
            total = jnp.zeros((16, DZ), F32)
            for q in range(NZ):
                part = mixed(p, rows, pl.ds(q * DZ, DZ))
                total = total + part * part
            mean = jnp.sum(total, axis=1, keepdims=True) * (1.0 / (NZ * DZ))
            inv[p, rows, :] = lax.rsqrt(mean + EPSILON)

    pl.when(swapped)(begin_ring)

    def h_copy(slot):
        return remote(hb.at[0, slot], hb.at[1, slot], s_h.at[slot], r_h.at[slot], partner)

    def distance(i):
        return lax.rem(i + 1, 2) * (-((i + 1) // 2)) + lax.rem(i, 2) * ((i + 1) // 2)

    def make_inputs(first, count):
        @pl.loop(first, first + count)
        def _(i):
            slot = at_z(distance(i))
            cols = pl.ds(pl.multiple_of(slot * DZ, 128), DZ)
            for p in range(2):

                @pl.loop(0, TOK // RB)
                def _(b, p=p):
                    start = pl.multiple_of(b * RB, RB)
                    rows = pl.ds(start, RB)
                    part = mixed(p, rows, cols) * inv[p, rows, :] * gain[:, cols] + shift[p : p + 1, cols]
                    hb[0, slot, pl.ds(p * TOK + start, RB), :] = part.astype(BF16)

            @pl.when(swapped)
            def _():
                h_copy(slot).start()

    acc[...] = jnp.zeros_like(acc)

    def multiply(index, slot):
        for j in range(3):
            from_sibling(index, slot, j).wait_recv()

        @pl.when(swapped)
        def _():
            h_copy(slot).wait_recv()

        @pl.loop(0, 3)
        def _(j):
            acc[j] += jnp.dot(hb[sel, slot], wbuf[slot, j], preferred_element_type=F32)

    groups = [[(0, 0)], [(1, -1), (2, 1)], [(3, -2), (4, 2)], [(5, -3), (6, 3)], [(7, 4)]]
    make_inputs(0, 2)
    for k in range(1, 5):
        for j in range(3):
            for direction in range(2):
                landing(direction, k, j).wait_recv()
                if k < 4:
                    ring(direction, k + 1, j).start()
                    index, step = groups[k][direction]
                    to_sibling(index, at_z(step), j).start()
            if k == 4:
                index, step = groups[k][0]
                to_sibling(index, at_z(step), j).start()
            if k == 1:
                make_inputs(2 + 2 * j, 2)
        for index, step in groups[k - 1]:
            multiply(index, at_z(step))
    for index, step in groups[4]:
        multiply(index, at_z(step))

    my_part = pl.ds(z * TOK, TOK)

    def unit_remote(u):
        return remote(
            units.at[u], ub.at[:, core, my_part], s_a.at[u], r_a.at[z], {"z": owner_of(u)}
        )

    def unit_local(u):
        return pltpu.make_async_copy(units.at[u], ub.at[:, core, my_part], r_a.at[z])

    for u in range(UNITS):
        p, h = u // 3, u % 3
        for j in range(3):
            units[u, j] = acc[j, p * TOK : (p + 1) * TOK, h * HD : (h + 1) * HD].astype(BF16)

        @pl.when(z == owner_of(u))
        def _(u=u):
            unit_local(u).start()

        @pl.when(z != owner_of(u))
        def _(u=u):
            unit_remote(u).start()

    def wo_tick(t, act):
        for half in range(2):
            delta = lax.rem(z - (half * 4 + y_lo * 2 + x // 2) + NZ, NZ)
            b = t - (jnp.minimum(delta, NZ - delta) + 1)

            @pl.when((b >= 0) & (b < 8))
            def _(half=half, delta=delta, b=b):
                slot, part = core * 4 + b // 2, lax.rem(b, 2)
                block = wo.at[half, slot, pl.ds(pl.multiple_of(part * (ROWS // 2), 16), ROWS // 2)]

                def copy(lane, device):
                    return remote(
                        block, block, s_wo.at[lane, half, b], r_wo.at[half, slot, part], device
                    )

                if act == "send":
                    copy(2, sibling).wait_recv()
                right = (delta <= 2) | ((delta == 3) & (b < 4))
                left = (delta == 0) | (delta >= 6) | ((delta == 5) & (b >= 4))
                for lane, go, device in ((0, right, {"z": at_z(1)}), (1, left, {"z": at_z(-1)})):

                    @pl.when(go)
                    def _(lane=lane, device=device):
                        if act == "send":
                            copy(lane, device).start()
                        else:
                            copy(lane, device).wait_send()

                if act == "send":
                    copy(2, sibling).start()
                else:
                    copy(2, sibling).wait_send()

    is_owner = lax.rem(z, 4) != 3
    mine = jnp.minimum(z - z // 4, UNITS - 1)
    mine_rows = pl.ds(pl.multiple_of((mine // 3) * TOK, TOK), TOK)
    mine_cols = pl.ds(pl.multiple_of(lax.rem(mine, 3) * HD, HD), HD)

    def arrived(source):
        block = ub.at[:, core, pl.ds(source * TOK, TOK)]
        return remote(block, block, s_a.at[0], r_a.at[source], sibling)

    def kv_to_sibling(source, which):
        block = ub.at[pl.ds(1, 2), which, pl.ds(source * TOK, TOK)]
        return remote(block, block, s_kv.at[source], r_kv.at[source], sibling)

    def o_remote(to):
        return remote(ob.at[to], att.at[f, mine_rows, mine_cols], s_o.at[to], r_o.at[mine], {"z": to})

    def o_local(to):
        return pltpu.make_async_copy(ob.at[to], att.at[f, mine_rows, mine_cols], r_o.at[mine])

    @pl.when(is_owner)
    def _():
        @pl.loop(0, NZ)
        def _(i):
            source = at_z(distance(i))
            arrived(source).wait_recv()
            kv_to_sibling(source, core).start()

        @pl.loop(0, NZ)
        def _(i):
            kv_to_sibling(at_z(distance(i)), 1 - core).wait_recv()

    wo_tick(1, "send")

    @pl.loop(0, NZ)
    def _(i):
        to = at_z(distance(NZ - 1 - i))

        @pl.when(is_owner)
        def _():
            queries = ub[0, core, pl.ds(pl.multiple_of(to * TOK, TOK), TOK), :]
            keys = ub[1].reshape(2 * NZ * TOK, HD)
            scores = lax.dot_general(
                queries, keys, (((1,), (1,)), ((), ())), preferred_element_type=F32
            )
            peak = jnp.max(scores, axis=1, keepdims=True)
            weight = jnp.exp2((scores - peak) * (HD**-0.5 * LOG2E))
            mass = jnp.sum(weight, axis=1, keepdims=True)
            result = jnp.dot(
                weight.astype(BF16), ub[2].reshape(2 * NZ * TOK, HD), preferred_element_type=F32
            )
            ob[to] = (result / mass).astype(BF16)

            @pl.when(to == z)
            def _():
                o_local(to).start()

            @pl.when(to != z)
            def _():
                o_remote(to).start()

        @pl.when(lax.rem(i, 2) == 1)
        def _():
            wo_tick(2 + i // 2, "send")

    other_f = (1 - y_lo) * 4 + x
    far_f = y_lo * 4 + lax.rem(x + 2, 4)
    x_up, x_down, x_far = ({"x": lax.rem(x + step, 4)} for step in (1, 3, 2))
    y_other = {"y_lo": 1 - y_lo}

    def att_copy(lane, source, p, device):
        block = att.at[source, pl.ds(p * TOK, TOK)]
        return remote(block, block, s_att.at[lane, p], r_att.at[source, p], device)

    def att_wait(source, p):
        att_copy(0, source, p, sibling).wait_recv()

    def att_first(p):
        return [
            att_copy(lane, f, p, device) for lane, device in enumerate((x_up, x_down, y_other, x_far))
        ]

    def att_second(p):
        return [att_copy(4, other_f, p, x_up), att_copy(5, other_f, p, x_down)]

    def att_third(p):
        return [att_copy(6, far_f, p, y_other)]

    for p in range(2):
        for h in range(3):
            block = att.at[f, pl.ds(p * TOK, TOK), pl.ds(h * HD, HD)]
            remote(block, block, s_o.at[0], r_o.at[p * 3 + h], sibling).wait_recv()
        for copy in att_first(p):
            copy.start()

    target_load.wait()
    difference = target[...].astype(F32) - lat[:, window].astype(F32)

    @pl.when(lax.rem(out_block, 2) == 0)
    def _():
        base[...] = difference[:, :ROWS]

    @pl.when(lax.rem(out_block, 2) == 1)
    def _():
        base[...] = difference[:, COLS - ROWS :]

    wo_tick(6, "send")
    for p in range(2):
        att_wait(other_f, p)
        for copy in att_second(p):
            copy.start()
        wo_tick(7 + p, "send")
    for p in range(2):
        att_wait(far_f, p)
        for copy in att_third(p):
            copy.start()
        wo_tick(9 + p, "send")
    wo_tick(11, "send")
    wo_tick(12, "send")

    pred[...] = jnp.zeros_like(pred)

    @pl.loop(0, 8)
    def _(step):
        source = at_f(step)

        @pl.when((source != f) & (source != other_f) & (source != far_f))
        def _():
            for p in range(2):
                att_wait(source, p)

        for half in range(2):

            @pl.when(source // 4 != core)
            def _(half=half):
                for part in range(2):
                    block = wo.at[half, source, wo_part(part)]
                    remote(
                        block, block, s_wo.at[2, half, 0], r_wo.at[half, source, part], sibling
                    ).wait_recv()

            pred[half] += lax.dot_general(
                att[source], wo[half, source], (((1,), (1,)), ((), ())), preferred_element_type=F32
            )

    def fin_copy(half):
        return remote(
            pb.at[half], fin.at[y_hi], s_f.at[half], r_f.at[y_hi], {"core": half, "y_hi": core}
        )

    for half in range(2):
        stays = (core == half) & (y_hi == core)
        pb[half] = pred[half].astype(BF16)

        @pl.when(stays)
        def _(half=half):
            pltpu.make_async_copy(pb.at[half], fin.at[y_hi], r_f.at[y_hi]).start()

        @pl.when(jnp.logical_not(stays))
        def _(half=half):
            fin_copy(half).start()

    for section in range(2):
        block = fin.at[section]
        remote(block, block, s_f.at[0], r_f.at[section], sibling).wait_recv()

    def found(section, p):
        return fin[section, p * TOK : (p + 1) * TOK, :].astype(F32)

    dmd[...] = found(1, 0) - (found(0, 1) + GUIDANCE * (found(0, 0) - found(0, 1)))
    residual[...] = found(1, 1) - base[...]

    @pl.when(swapped)
    def _():
        for j in range(3):
            own_remote(j).wait_send()
        for slot in range(NZ):
            h_copy(slot).wait_send()

    @pl.when(jnp.logical_not(in_place))
    def _():
        for part in range(2):
            wo_in(part).wait_send()

    for k in range(1, 5):
        for j in range(3):
            for direction in range(2):
                ring(direction, k, j).wait_send()
    for group in groups:
        for index, step in group:
            for j in range(3):
                to_sibling(index, at_z(step), j).wait_send()
    for u in range(UNITS):

        @pl.when(z != owner_of(u))
        def _(u=u):
            unit_remote(u).wait_send()

    @pl.when(is_owner)
    def _():
        for source in range(NZ):
            kv_to_sibling(source, core).wait_send()

            @pl.when(z != source)
            def _(source=source):
                o_remote(source).wait_send()

    @pl.loop(1, 13)
    def _(t):
        wo_tick(t, "wait")

    for p in range(2):
        for copy in att_first(p) + att_second(p) + att_third(p):
            copy.wait_send()
    for half in range(2):

        @pl.when(jnp.logical_not((core == half) & (y_hi == core)))
        def _(half=half):
            fin_copy(half).wait_send()


def outputs(times, pair, latents, noise, cond_table, gain, w_qkv, w_out):
    dma = pltpu.SemaphoreType.DMA
    vmem, any_space = pl.BlockSpec(memory_space=pltpu.VMEM), pl.BlockSpec(memory_space=pl.ANY)
    smem = pl.BlockSpec(memory_space=pltpu.SMEM)
    return pl.pallas_call(
        step_kernel,
        out_shape=[jax.ShapeDtypeStruct((TOK, ROWS), F32)] * 2,
        in_specs=[smem, smem, any_space, any_space, vmem, vmem, any_space, any_space],
        out_specs=[vmem, vmem],
        scratch_shapes=[
            pltpu.VMEM((TOK, NZ * DZ), BF16),
            pltpu.VMEM((2, TOK, NZ * DZ), BF16),
            pltpu.VMEM((2, NZ * DZ), F32),
            pltpu.VMEM((2, NZ, 2 * TOK, DZ), BF16),
            pltpu.VMEM((2, TOK, 1), F32),
            pltpu.VMEM((NZ, 3, DZ, COLS), BF16),
            pltpu.VMEM((3, 2 * TOK, COLS), F32),
            pltpu.VMEM((UNITS, 3, TOK, HD), BF16),
            pltpu.VMEM((3, 2, NZ * TOK, HD), BF16),
            pltpu.VMEM((NZ, TOK, HD), BF16),
            pltpu.VMEM((8, 2 * TOK, COLS), BF16),
            pltpu.VMEM((2, 8, ROWS, COLS), BF16),
            pltpu.VMEM((2, 2 * TOK, ROWS), F32),
            pltpu.VMEM((2, 2 * TOK, ROWS), BF16),
            pltpu.VMEM((2, 2 * TOK, ROWS), BF16),
            pltpu.VMEM((TOK, COLS), BF16),
            pltpu.VMEM((TOK, ROWS), F32),
            dma((4,)),
            dma((3,)), dma((3,)),
            dma((NZ,)), dma((NZ,)),
            dma((2, 4, 3)), dma((2, 4, 3)),
            dma((NZ, 3)), dma((NZ, 3)),
            dma((UNITS,)), dma((NZ,)),
            dma((NZ,)), dma((NZ,)),
            dma((NZ,)), dma((UNITS,)),
            dma((2,)), dma((3, 2, 8)), dma((2, 8, 2)),
            dma((7, 2)), dma((8, 2)),
            dma((2,)), dma((2,)),
        ],
        compiler_params=pltpu.CompilerParams(
            collective_id=0, has_side_effects=True, vmem_limit_bytes=60 * 2**20
        ),
        cost_estimate=pl.CostEstimate(
            flops=9_000_000_000, bytes_accessed=40_000_000, transcendentals=5_000_000
        ),
    )(times, pair, latents, noise, cond_table, gain, w_qkv, w_out)


def body(latents, noise, time_index, cfg_pair, cond_table, gain, w_qkv, w_out):
    return tuple(
        outputs(
            time_index, cfg_pair, latents, noise, cond_table, gain, w_qkv, jnp.swapaxes(w_out[0], 0, 1)
        )
    )


def solution(mesh):
    torus = Mesh(mesh.devices.reshape(2, NZ, 2, 2, 4), AXES)
    seq, fsdp = ("z", "y_hi"), ("y_lo", "x")
    return jax.shard_map(
        body,
        mesh=torus,
        in_specs=(
            P(seq, None),
            P(None, seq, None),
            P(),
            P(),
            P(),
            P("core", None),
            P("core", None, seq, fsdp),
            P("core", fsdp, seq),
        ),
        out_specs=(P(seq, ("core", *fsdp)), P(seq, ("core", *fsdp))),
        check_vma=False,
    )
```

```python
import functools

import jax
import jax.numpy as jnp
from jax import lax
from jax.experimental import pallas as pl
from jax.experimental.pallas import tpu as pltpu
from jax.sharding import Mesh
from jax.sharding import PartitionSpec as P

HD = 128
LOG2E = 1.4426950408889634
GUIDANCE = 3.5
EPSILON = 1e-06
MESH = pl.DeviceIdType.MESH
BF16, F32 = jnp.bfloat16, jnp.float32

AXES = ("core", "z", "y_hi", "y_lo", "x")
NZ = 8
TOK = 192
DZ = 640
ROWS = 320
COLS = 384
UNITS = 6
RB = 64


def owner_of(unit):
    return unit + unit // 3


def step_kernel(
    times, pair, lat_hbm, noise_hbm, cond, gain, w_hbm, wo_hbm, dmd, residual,
    lat, noi, shift, hb, inv, wbuf, acc, units, ub, ob, att, wr, wo, pred, pb, fin, target, base,
    s_in, s_w, r_w, s_h, r_h, s_ring, r_ring, s_sib, r_sib, s_a, r_a, s_kv, r_kv, s_o, r_o,
    s_wr, r_wr, s_wo, r_wo, s_ws, s_att, r_att, s_f, r_f,
):
    core, z, y_hi = lax.axis_index("core"), lax.axis_index("z"), lax.axis_index("y_hi")
    y_lo, x = lax.axis_index("y_lo"), lax.axis_index("x")
    f = y_lo * 4 + x
    swapped = core != y_hi
    sel = lax.rem(core + y_hi, 2)
    partner = {"core": 1 - core, "y_hi": 1 - y_hi}
    sibling = {"core": 1 - core}

    def at_z(step):
        return lax.rem(z + step + NZ, NZ)

    def at_f(step):
        return lax.rem(f + step, 8)

    def f_device(peer):
        return {"y_lo": peer // 4, "x": lax.rem(peer, 4)}

    def remote(src, dst, send, recv, device):
        return pltpu.make_async_remote_copy(
            src_ref=src, dst_ref=dst, send_sem=send, recv_sem=recv, device_id=device, device_id_type=MESH
        )

    loads = [
        pltpu.make_async_copy(lat_hbm, lat, s_in.at[0]),
        pltpu.make_async_copy(noise_hbm.at[0], noi.at[0], s_in.at[1]),
        pltpu.make_async_copy(noise_hbm.at[core], noi.at[1], s_in.at[2]),
    ]
    out_block = core * 8 + f
    window = pl.ds(pl.multiple_of(((out_block * 5) // 2) * 128, 128), COLS)
    target_load = pltpu.make_async_copy(noise_hbm.at[1, :, window], target, s_in.at[3])
    target_load.start()
    for load in loads:
        load.start()

    barrier = pltpu.get_barrier_semaphore()

    def greet(device):
        pl.semaphore_signal(barrier, inc=1, device_id=device, device_id_type=MESH)

    greet(partner)
    greet(sibling)
    greet({"y_hi": 1 - y_hi})
    for step in range(1, NZ):
        greet({"z": at_z(step)})
    for step in range(1, 8):
        greet(f_device(at_f(step)))
    same = lax.rem(x, 2) == core

    @pl.when(jnp.logical_not(same))
    def _():
        for step in range(1, 8):
            greet({"core": 1 - core, **f_device(at_f(step))})

    @pl.when(same)
    def _():
        pl.semaphore_wait(barrier, 20)

    @pl.when(jnp.logical_not(same))
    def _():
        pl.semaphore_wait(barrier, 21)

    my_rows = pl.ds(core * ROWS, ROWS)
    sib_rows = pl.ds((1 - core) * ROWS, ROWS)

    def own_local(j):
        return pltpu.make_async_copy(w_hbm.at[0, j], wbuf.at[z, j, my_rows], r_w.at[j])

    def own_remote(j):
        return remote(
            w_hbm.at[0, j], wbuf.at[z, j, pl.ds(y_hi * ROWS, ROWS)], s_w.at[j], r_w.at[j], partner
        )

    def wr_own_local():
        return pltpu.make_async_copy(wo_hbm, wr.at[z], r_wr.at[0, 0])

    def wr_own_remote():
        return remote(wo_hbm, wr.at[z], s_wr.at[0, 0], r_wr.at[0, 0], partner)

    @pl.when(swapped)
    def _():
        for j in range(3):
            own_remote(j).start()
        wr_own_remote().start()

    @pl.when(jnp.logical_not(swapped))
    def _():
        for j in range(3):
            own_local(j).start()
        wr_own_local().start()

    def ring_copy(direction, k, j, moved):
        sign = 1 - 2 * direction
        slot = at_z(-sign * (k - 1 + moved))
        if k < 4:
            rows = my_rows
        else:
            rows = pl.ds(core * ROWS + direction * (ROWS // 2), ROWS // 2)
        block = wbuf.at[slot, j, rows]
        return remote(
            block, block, s_ring.at[direction, k - 1, j], r_ring.at[direction, k - 1, j], {"z": at_z(sign)}
        )

    def ring(direction, k, j):
        return ring_copy(direction, k, j, 0)

    def landing(direction, k, j):
        return ring_copy(direction, k, j, 1)

    def to_sibling(index, slot, j):
        block = wbuf.at[slot, j, my_rows]
        return remote(block, block, s_sib.at[index, j], r_sib.at[index, j], sibling)

    def from_sibling(index, slot, j):
        block = wbuf.at[slot, j, sib_rows]
        return remote(block, block, s_sib.at[index, j], r_sib.at[index, j], sibling)

    def begin_ring():
        for j in range(3):
            own_local(j).wait()
            ring(0, 1, j).start()
            ring(1, 1, j).start()
            to_sibling(0, z, j).start()

    pl.when(jnp.logical_not(swapped))(begin_ring)

    def wr_copy(direction, k, moved):
        sign = 1 - 2 * direction
        slot = at_z(-sign * (k - 1 + moved))
        rows = pl.ds(0, ROWS) if k < 4 else pl.ds(direction * (ROWS // 2), ROWS // 2)
        block = wr.at[slot, rows]
        return remote(block, block, s_wr.at[direction, k], r_wr.at[direction, k], {"z": at_z(sign)})

    def wr_out(slot, act):
        half, to = slot // 4, 2 * lax.rem(slot, 4) + core
        here = (to == f) & (half == core)

        @pl.when(jnp.logical_not(here))
        def _():
            copy = remote(
                wr.at[slot], wo.at[half, f], s_wo.at[slot], r_wo.at[half, f],
                {"core": half, **f_device(to)},
            )
            if act == "send":
                copy.start()
            else:
                copy.wait_send()

        if act == "send":

            @pl.when(here)
            def _():
                pltpu.make_async_copy(wr.at[slot], wo.at[half, f], r_wo.at[half, f]).start()

    def wr_begin():
        wr_own_local().wait()
        wr_copy(0, 1, 0).start()
        wr_copy(1, 1, 0).start()
        wr_out(z, "send")

    def wr_step(k):
        for direction in range(2):
            wr_copy(direction, k, 1).wait_recv()
            if k < 4:
                wr_copy(direction, k + 1, 0).start()
                wr_out(at_z((2 * direction - 1) * k), "send")
        if k == 4:
            wr_out(at_z(4), "send")

    def wo_share(source):
        block = wo.at[core, source]
        return remote(block, block, s_ws.at[source], r_wo.at[core, source], sibling)

    def wo_forward(source):
        wo_share(source).wait_recv()
        wo_share(source).start()

    def level_of(step_index):
        fraction = jnp.full((8, 128), step_index.astype(F32)) / 1000.0
        return (5.0 * fraction / (1.0 + 4.0 * fraction))[0:1, 0:1]

    levels = (level_of(times[0]), level_of(times[core]))
    shift[0:1, :] = cond[pl.ds(pair[0], 1), :]
    shift[1:2, :] = cond[pl.ds(pair[1 - core], 1), :]
    for load in loads:
        load.wait()

    def mixed(p, rows, cols):
        return (1.0 - levels[p]) * lat[rows, cols].astype(F32) + levels[p] * noi[p, rows, cols].astype(F32)

    for p in range(2):

        @pl.loop(0, TOK // 16)
        def _(b, p=p):
            rows = pl.ds(pl.multiple_of(b * 16, 16), 16)
            total = jnp.zeros((16, DZ), F32)
            for q in range(NZ):
                part = mixed(p, rows, pl.ds(q * DZ, DZ))
                total = total + part * part
            mean = jnp.sum(total, axis=1, keepdims=True) * (1.0 / (NZ * DZ))
            inv[p, rows, :] = lax.rsqrt(mean + EPSILON)

    pl.when(swapped)(begin_ring)

    def h_copy(slot):
        return remote(hb.at[0, slot], hb.at[1, slot], s_h.at[slot], r_h.at[slot], partner)

    def distance(i):
        return lax.rem(i + 1, 2) * (-((i + 1) // 2)) + lax.rem(i, 2) * ((i + 1) // 2)

    def make_inputs(first, count):
        @pl.loop(first, first + count)
        def _(i):
            slot = at_z(distance(i))
            cols = pl.ds(pl.multiple_of(slot * DZ, 128), DZ)
            for p in range(2):

                @pl.loop(0, TOK // RB)
                def _(b, p=p):
                    start = pl.multiple_of(b * RB, RB)
                    rows = pl.ds(start, RB)
                    part = mixed(p, rows, cols) * inv[p, rows, :] * gain[:, cols] + shift[p : p + 1, cols]
                    hb[0, slot, pl.ds(p * TOK + start, RB), :] = part.astype(BF16)

            @pl.when(swapped)
            def _():
                h_copy(slot).start()

    acc[...] = jnp.zeros_like(acc)

    def multiply(index, slot):
        for j in range(3):
            from_sibling(index, slot, j).wait_recv()

        @pl.when(swapped)
        def _():
            h_copy(slot).wait_recv()

        @pl.loop(0, 3)
        def _(j):
            acc[j] += jnp.dot(hb[sel, slot], wbuf[slot, j], preferred_element_type=F32)

    groups = [[(0, 0)], [(1, -1), (2, 1)], [(3, -2), (4, 2)], [(5, -3), (6, 3)], [(7, 4)]]
    make_inputs(0, 2)
    for k in range(1, 5):
        for j in range(3):
            for direction in range(2):
                landing(direction, k, j).wait_recv()
                if k < 4:
                    ring(direction, k + 1, j).start()
                    index, step = groups[k][direction]
                    to_sibling(index, at_z(step), j).start()
            if k == 4:
                index, step = groups[k][0]
                to_sibling(index, at_z(step), j).start()
            if k == 1:
                make_inputs(2 + 2 * j, 2)
        if k == 3:
            wr_begin()
        if k == 4:
            wr_step(1)
        for index, step in groups[k - 1]:
            multiply(index, at_z(step))
    for index, step in groups[4]:
        multiply(index, at_z(step))

    my_part = pl.ds(z * TOK, TOK)

    def unit_remote(u):
        return remote(
            units.at[u], ub.at[:, core, my_part], s_a.at[u], r_a.at[z], {"z": owner_of(u)}
        )

    def unit_local(u):
        return pltpu.make_async_copy(units.at[u], ub.at[:, core, my_part], r_a.at[z])

    for u in range(UNITS):
        p, h = u // 3, u % 3
        for j in range(3):
            units[u, j] = acc[j, p * TOK : (p + 1) * TOK, h * HD : (h + 1) * HD].astype(BF16)

        @pl.when(z == owner_of(u))
        def _(u=u):
            unit_local(u).start()

        @pl.when(z != owner_of(u))
        def _(u=u):
            unit_remote(u).start()

    wr_step(2)
    is_owner = lax.rem(z, 4) != 3
    mine = jnp.minimum(z - z // 4, UNITS - 1)
    mine_rows = pl.ds(pl.multiple_of((mine // 3) * TOK, TOK), TOK)
    mine_cols = pl.ds(pl.multiple_of(lax.rem(mine, 3) * HD, HD), HD)

    def arrived(source):
        block = ub.at[:, core, pl.ds(source * TOK, TOK)]
        return remote(block, block, s_a.at[0], r_a.at[source], sibling)

    def kv_to_sibling(source, which):
        block = ub.at[pl.ds(1, 2), which, pl.ds(source * TOK, TOK)]
        return remote(block, block, s_kv.at[source], r_kv.at[source], sibling)

    def o_remote(to):
        return remote(ob.at[to], att.at[f, mine_rows, mine_cols], s_o.at[to], r_o.at[mine], {"z": to})

    def o_local(to):
        return pltpu.make_async_copy(ob.at[to], att.at[f, mine_rows, mine_cols], r_o.at[mine])

    @pl.when(is_owner)
    def _():
        @pl.loop(0, NZ)
        def _(i):
            source = at_z(distance(i))
            arrived(source).wait_recv()
            kv_to_sibling(source, core).start()

        @pl.loop(0, NZ)
        def _(i):
            kv_to_sibling(at_z(distance(i)), 1 - core).wait_recv()


    wr_step(3)

    @pl.loop(0, NZ)
    def _(i):
        to = at_z(distance(NZ - 1 - i))

        @pl.when(is_owner)
        def _():
            queries = ub[0, core, pl.ds(pl.multiple_of(to * TOK, TOK), TOK), :]
            keys = ub[1].reshape(2 * NZ * TOK, HD)
            scores = lax.dot_general(
                queries, keys, (((1,), (1,)), ((), ())), preferred_element_type=F32
            )
            peak = jnp.max(scores, axis=1, keepdims=True)
            weight = jnp.exp2((scores - peak) * (HD**-0.5 * LOG2E))
            mass = jnp.sum(weight, axis=1, keepdims=True)
            result = jnp.dot(
                weight.astype(BF16), ub[2].reshape(2 * NZ * TOK, HD), preferred_element_type=F32
            )
            ob[to] = (result / mass).astype(BF16)

            @pl.when(to == z)
            def _():
                o_local(to).start()

            @pl.when(to != z)
            def _():
                o_remote(to).start()

        pl.when(i == 3)(functools.partial(wr_step, 4))

    other_f = (1 - y_lo) * 4 + x
    far_f = y_lo * 4 + lax.rem(x + 2, 4)
    x_up, x_down, x_far = ({"x": lax.rem(x + step, 4)} for step in (1, 3, 2))
    y_other = {"y_lo": 1 - y_lo}

    def att_copy(lane, source, p, device):
        block = att.at[source, pl.ds(p * TOK, TOK)]
        return remote(block, block, s_att.at[lane, p], r_att.at[source, p], device)

    def att_wait(source, p):
        att_copy(0, source, p, sibling).wait_recv()

    def att_first(p):
        return [
            att_copy(lane, f, p, device) for lane, device in enumerate((x_up, x_down, y_other, x_far))
        ]

    def att_second(p):
        return [att_copy(4, other_f, p, x_up), att_copy(5, other_f, p, x_down)]

    def att_third(p):
        return [att_copy(6, far_f, p, y_other)]

    for p in range(2):
        for h in range(3):
            block = att.at[f, pl.ds(p * TOK, TOK), pl.ds(h * HD, HD)]
            remote(block, block, s_o.at[0], r_o.at[p * 3 + h], sibling).wait_recv()
        for copy in att_first(p):
            copy.start()

    target_load.wait()
    difference = target[...].astype(F32) - lat[:, window].astype(F32)

    @pl.when(lax.rem(out_block, 2) == 0)
    def _():
        base[...] = difference[:, :ROWS]

    @pl.when(lax.rem(out_block, 2) == 1)
    def _():
        base[...] = difference[:, COLS - ROWS :]

    for p in range(2):
        att_wait(other_f, p)
        for copy in att_second(p):
            copy.start()
    for p in range(2):
        att_wait(far_f, p)
        for copy in att_third(p):
            copy.start()

    @pl.loop(0, 8)
    def _(source):
        wo_forward(source)

    pred[...] = jnp.zeros_like(pred)

    @pl.loop(0, 8)
    def _(step):
        source = at_f(step)

        @pl.when((source != f) & (source != other_f) & (source != far_f))
        def _():
            for p in range(2):
                att_wait(source, p)

        block = wo.at[1 - core, source]
        remote(block, block, s_ws.at[source], r_wo.at[1 - core, source], sibling).wait_recv()
        for half in range(2):
            pred[half] += lax.dot_general(
                att[source], wo[half, source], (((1,), (1,)), ((), ())), preferred_element_type=F32
            )

    def fin_copy(half):
        return remote(
            pb.at[half], fin.at[y_hi], s_f.at[half], r_f.at[y_hi], {"core": half, "y_hi": core}
        )

    for half in range(2):
        stays = (core == half) & (y_hi == core)
        pb[half] = pred[half].astype(BF16)

        @pl.when(stays)
        def _(half=half):
            pltpu.make_async_copy(pb.at[half], fin.at[y_hi], r_f.at[y_hi]).start()

        @pl.when(jnp.logical_not(stays))
        def _(half=half):
            fin_copy(half).start()

    for section in range(2):
        block = fin.at[section]
        remote(block, block, s_f.at[0], r_f.at[section], sibling).wait_recv()

    def found(section, p):
        return fin[section, p * TOK : (p + 1) * TOK, :].astype(F32)

    dmd[...] = found(1, 0) - (found(0, 1) + GUIDANCE * (found(0, 0) - found(0, 1)))
    residual[...] = found(1, 1) - base[...]

    @pl.when(swapped)
    def _():
        for j in range(3):
            own_remote(j).wait_send()
        wr_own_remote().wait_send()
        for slot in range(NZ):
            h_copy(slot).wait_send()

    for slot in range(NZ):
        wr_out(slot, "wait")
        wo_share(slot).wait_send()
    for k in range(1, 5):
        for direction in range(2):
            wr_copy(direction, k, 0).wait_send()
    for k in range(1, 5):
        for j in range(3):
            for direction in range(2):
                ring(direction, k, j).wait_send()
    for group in groups:
        for index, step in group:
            for j in range(3):
                to_sibling(index, at_z(step), j).wait_send()
    for u in range(UNITS):

        @pl.when(z != owner_of(u))
        def _(u=u):
            unit_remote(u).wait_send()

    @pl.when(is_owner)
    def _():
        for source in range(NZ):
            kv_to_sibling(source, core).wait_send()

            @pl.when(z != source)
            def _(source=source):
                o_remote(source).wait_send()

    for p in range(2):
        for copy in att_first(p) + att_second(p) + att_third(p):
            copy.wait_send()
    for half in range(2):

        @pl.when(jnp.logical_not((core == half) & (y_hi == core)))
        def _(half=half):
            fin_copy(half).wait_send()


def outputs(times, pair, latents, noise, cond_table, gain, w_qkv, w_out):
    dma = pltpu.SemaphoreType.DMA
    vmem, any_space = pl.BlockSpec(memory_space=pltpu.VMEM), pl.BlockSpec(memory_space=pl.ANY)
    smem = pl.BlockSpec(memory_space=pltpu.SMEM)
    return pl.pallas_call(
        step_kernel,
        out_shape=[jax.ShapeDtypeStruct((TOK, ROWS), F32)] * 2,
        in_specs=[smem, smem, any_space, any_space, vmem, vmem, any_space, any_space],
        out_specs=[vmem, vmem],
        scratch_shapes=[
            pltpu.VMEM((TOK, NZ * DZ), BF16),
            pltpu.VMEM((2, TOK, NZ * DZ), BF16),
            pltpu.VMEM((2, NZ * DZ), F32),
            pltpu.VMEM((2, NZ, 2 * TOK, DZ), BF16),
            pltpu.VMEM((2, TOK, 1), F32),
            pltpu.VMEM((NZ, 3, DZ, COLS), BF16),
            pltpu.VMEM((3, 2 * TOK, COLS), F32),
            pltpu.VMEM((UNITS, 3, TOK, HD), BF16),
            pltpu.VMEM((3, 2, NZ * TOK, HD), BF16),
            pltpu.VMEM((NZ, TOK, HD), BF16),
            pltpu.VMEM((8, 2 * TOK, COLS), BF16),
            pltpu.VMEM((NZ, ROWS, COLS), BF16),
            pltpu.VMEM((2, 8, ROWS, COLS), BF16),
            pltpu.VMEM((2, 2 * TOK, ROWS), F32),
            pltpu.VMEM((2, 2 * TOK, ROWS), BF16),
            pltpu.VMEM((2, 2 * TOK, ROWS), BF16),
            pltpu.VMEM((TOK, COLS), BF16),
            pltpu.VMEM((TOK, ROWS), F32),
            dma((4,)),
            dma((3,)), dma((3,)),
            dma((NZ,)), dma((NZ,)),
            dma((2, 4, 3)), dma((2, 4, 3)),
            dma((NZ, 3)), dma((NZ, 3)),
            dma((UNITS,)), dma((NZ,)),
            dma((NZ,)), dma((NZ,)),
            dma((NZ,)), dma((UNITS,)),
            dma((2, 5)), dma((2, 5)), dma((NZ,)), dma((2, 8)), dma((8,)),
            dma((7, 2)), dma((8, 2)),
            dma((2,)), dma((2,)),
        ],
        compiler_params=pltpu.CompilerParams(
            collective_id=0, has_side_effects=True, vmem_limit_bytes=60 * 2**20
        ),
        cost_estimate=pl.CostEstimate(
            flops=9_000_000_000, bytes_accessed=40_000_000, transcendentals=5_000_000
        ),
    )(times, pair, latents, noise, cond_table, gain, w_qkv, w_out)


def body(latents, noise, time_index, cfg_pair, cond_table, gain, w_qkv, w_out):
    return tuple(
        outputs(
            time_index, cfg_pair, latents, noise, cond_table, gain, w_qkv, jnp.swapaxes(w_out[0], 0, 1)
        )
    )


def solution(mesh):
    torus = Mesh(mesh.devices.reshape(2, NZ, 2, 2, 4), AXES)
    seq, fsdp = ("z", "y_hi"), ("y_lo", "x")
    return jax.shard_map(
        body,
        mesh=torus,
        in_specs=(
            P(seq, None),
            P(None, seq, None),
            P(),
            P(),
            P(),
            P("core", None),
            P("core", None, seq, fsdp),
            P("core", fsdp, seq),
        ),
        out_specs=(P(seq, ("core", *fsdp)), P(seq, ("core", *fsdp))),
        check_vma=False,
    )
```

```python
import functools

import jax
import jax.numpy as jnp
from jax import lax
from jax.experimental import pallas as pl
from jax.experimental.pallas import tpu as pltpu
from jax.sharding import Mesh
from jax.sharding import PartitionSpec as P

HD = 128
LOG2E = 1.4426950408889634
GUIDANCE = 3.5
EPSILON = 1e-06
MESH = pl.DeviceIdType.MESH
BF16, F32 = jnp.bfloat16, jnp.float32

AXES = ("core", "z", "y_hi", "y_lo", "x")
NZ = 8
TOK = 192
DZ = 640
ROWS = 320
COLS = 384
UNITS = 6
RB = 64


def owner_of(unit):
    return unit + unit // 3


def step_kernel(
    times, pair, lat_hbm, noise_hbm, cond, gain, w_hbm, wo_hbm, dmd, residual,
    lat, noi, shift, hb, inv, wbuf, acc, units, ub, ob, att, wr, wo, pred, pb, fin, target, base,
    s_in, s_w, r_w, s_h, r_h, s_ring, r_ring, s_sib, r_sib, s_a, r_a, s_kv, r_kv, s_o, r_o,
    s_wr, r_wr, s_wo, r_wo, s_ws, s_att, r_att, s_f, r_f,
):
    core, z, y_hi = lax.axis_index("core"), lax.axis_index("z"), lax.axis_index("y_hi")
    y_lo, x = lax.axis_index("y_lo"), lax.axis_index("x")
    f = y_lo * 4 + x
    swapped = core != y_hi
    sel = lax.rem(core + y_hi, 2)
    partner = {"core": 1 - core, "y_hi": 1 - y_hi}
    sibling = {"core": 1 - core}

    def at_z(step):
        return lax.rem(z + step + NZ, NZ)

    def at_f(step):
        return lax.rem(f + step, 8)

    def f_device(peer):
        return {"y_lo": peer // 4, "x": lax.rem(peer, 4)}

    def remote(src, dst, send, recv, device):
        return pltpu.make_async_remote_copy(
            src_ref=src, dst_ref=dst, send_sem=send, recv_sem=recv, device_id=device, device_id_type=MESH
        )

    loads = [
        pltpu.make_async_copy(lat_hbm, lat, s_in.at[0]),
        pltpu.make_async_copy(noise_hbm.at[0], noi.at[0], s_in.at[1]),
        pltpu.make_async_copy(noise_hbm.at[core], noi.at[1], s_in.at[2]),
    ]
    out_block = core * 8 + f
    window = pl.ds(pl.multiple_of(((out_block * 5) // 2) * 128, 128), COLS)
    target_load = pltpu.make_async_copy(noise_hbm.at[1, :, window], target, s_in.at[3])
    target_load.start()
    for load in loads:
        load.start()

    barrier = pltpu.get_barrier_semaphore()

    def greet(device):
        pl.semaphore_signal(barrier, inc=1, device_id=device, device_id_type=MESH)

    greet(partner)
    greet(sibling)
    greet({"y_hi": 1 - y_hi})
    for step in range(1, NZ):
        greet({"z": at_z(step)})
    for step in range(1, 8):
        greet(f_device(at_f(step)))
    same = lax.rem(x, 2) == core

    @pl.when(jnp.logical_not(same))
    def _():
        for step in range(1, 8):
            greet({"core": 1 - core, **f_device(at_f(step))})

    @pl.when(same)
    def _():
        pl.semaphore_wait(barrier, 20)

    @pl.when(jnp.logical_not(same))
    def _():
        pl.semaphore_wait(barrier, 21)

    my_rows = pl.ds(core * ROWS, ROWS)
    sib_rows = pl.ds((1 - core) * ROWS, ROWS)

    def own_local(j):
        return pltpu.make_async_copy(w_hbm.at[0, j], wbuf.at[z, j, my_rows], r_w.at[j])

    def own_remote(j):
        return remote(
            w_hbm.at[0, j], wbuf.at[z, j, pl.ds(y_hi * ROWS, ROWS)], s_w.at[j], r_w.at[j], partner
        )

    def wr_own_local():
        return pltpu.make_async_copy(wo_hbm, wr.at[z], r_wr.at[0, 0])

    def wr_own_remote():
        return remote(wo_hbm, wr.at[z], s_wr.at[0, 0], r_wr.at[0, 0], partner)

    @pl.when(swapped)
    def _():
        for j in range(3):
            own_remote(j).start()
        wr_own_remote().start()

    @pl.when(jnp.logical_not(swapped))
    def _():
        for j in range(3):
            own_local(j).start()
        wr_own_local().start()

    def ring_copy(direction, k, j, moved):
        sign = 1 - 2 * direction
        slot = at_z(-sign * (k - 1 + moved))
        if k < 4:
            rows = my_rows
        else:
            rows = pl.ds(core * ROWS + direction * (ROWS // 2), ROWS // 2)
        block = wbuf.at[slot, j, rows]
        return remote(
            block, block, s_ring.at[direction, k - 1, j], r_ring.at[direction, k - 1, j], {"z": at_z(sign)}
        )

    def ring(direction, k, j):
        return ring_copy(direction, k, j, 0)

    def landing(direction, k, j):
        return ring_copy(direction, k, j, 1)

    def to_sibling(index, slot, j):
        block = wbuf.at[slot, j, my_rows]
        return remote(block, block, s_sib.at[index, j], r_sib.at[index, j], sibling)

    def from_sibling(index, slot, j):
        block = wbuf.at[slot, j, sib_rows]
        return remote(block, block, s_sib.at[index, j], r_sib.at[index, j], sibling)

    def begin_ring():
        for j in range(3):
            own_local(j).wait()
            ring(0, 1, j).start()
            ring(1, 1, j).start()
            to_sibling(0, z, j).start()

    pl.when(jnp.logical_not(swapped))(begin_ring)

    def wr_copy(direction, k, moved):
        sign = 1 - 2 * direction
        slot = at_z(-sign * (k - 1 + moved))
        rows = pl.ds(0, ROWS) if k < 4 else pl.ds(direction * (ROWS // 2), ROWS // 2)
        block = wr.at[slot, rows]
        return remote(block, block, s_wr.at[direction, k], r_wr.at[direction, k], {"z": at_z(sign)})

    def wr_out(slot, act):
        half, to = slot // 4, 2 * lax.rem(slot, 4) + core
        here = (to == f) & (half == core)

        @pl.when(jnp.logical_not(here))
        def _():
            copy = remote(
                wr.at[slot], wo.at[half, f], s_wo.at[slot], r_wo.at[half, f],
                {"core": half, **f_device(to)},
            )
            if act == "send":
                copy.start()
            else:
                copy.wait_send()

        if act == "send":

            @pl.when(here)
            def _():
                pltpu.make_async_copy(wr.at[slot], wo.at[half, f], r_wo.at[half, f]).start()

    def wr_begin():
        wr_own_local().wait()
        wr_copy(0, 1, 0).start()
        wr_copy(1, 1, 0).start()
        wr_out(z, "send")

    def wr_step(k):
        for direction in range(2):
            wr_copy(direction, k, 1).wait_recv()
            if k < 4:
                wr_copy(direction, k + 1, 0).start()
                wr_out(at_z((2 * direction - 1) * k), "send")
        if k == 4:
            wr_out(at_z(4), "send")

    def wo_share(source):
        block = wo.at[core, source]
        return remote(block, block, s_ws.at[source], r_wo.at[core, source], sibling)

    def wo_forward(source):
        wo_share(source).wait_recv()
        wo_share(source).start()

    def level_of(step_index):
        fraction = jnp.full((8, 128), step_index.astype(F32)) / 1000.0
        return (5.0 * fraction / (1.0 + 4.0 * fraction))[0:1, 0:1]

    levels = (level_of(times[0]), level_of(times[core]))
    shift[0:1, :] = cond[pl.ds(pair[0], 1), :]
    shift[1:2, :] = cond[pl.ds(pair[1 - core], 1), :]
    for load in loads:
        load.wait()

    def mixed(p, rows, cols):
        return (1.0 - levels[p]) * lat[rows, cols].astype(F32) + levels[p] * noi[p, rows, cols].astype(F32)

    for p in range(2):

        @pl.loop(0, TOK // 16)
        def _(b, p=p):
            rows = pl.ds(pl.multiple_of(b * 16, 16), 16)
            total = jnp.zeros((16, DZ), F32)
            for q in range(NZ):
                part = mixed(p, rows, pl.ds(q * DZ, DZ))
                total = total + part * part
            mean = jnp.sum(total, axis=1, keepdims=True) * (1.0 / (NZ * DZ))
            inv[p, rows, :] = lax.rsqrt(mean + EPSILON)

    pl.when(swapped)(begin_ring)

    def h_copy(slot):
        return remote(hb.at[0, slot], hb.at[1, slot], s_h.at[slot], r_h.at[slot], partner)

    def distance(i):
        return lax.rem(i + 1, 2) * (-((i + 1) // 2)) + lax.rem(i, 2) * ((i + 1) // 2)

    def make_inputs(first, count):
        @pl.loop(first, first + count)
        def _(i):
            slot = at_z(distance(i))
            cols = pl.ds(pl.multiple_of(slot * DZ, 128), DZ)
            for p in range(2):

                @pl.loop(0, TOK // RB)
                def _(b, p=p):
                    start = pl.multiple_of(b * RB, RB)
                    rows = pl.ds(start, RB)
                    part = mixed(p, rows, cols) * inv[p, rows, :] * gain[:, cols] + shift[p : p + 1, cols]
                    hb[0, slot, pl.ds(p * TOK + start, RB), :] = part.astype(BF16)

            @pl.when(swapped)
            def _():
                h_copy(slot).start()

    acc[...] = jnp.zeros_like(acc)

    def multiply(index, slot):
        for j in range(3):
            from_sibling(index, slot, j).wait_recv()

        @pl.when(swapped)
        def _():
            h_copy(slot).wait_recv()

        @pl.loop(0, 3)
        def _(j):
            acc[j] += jnp.dot(hb[sel, slot], wbuf[slot, j], preferred_element_type=F32)

    groups = [[(0, 0)], [(1, -1), (2, 1)], [(3, -2), (4, 2)], [(5, -3), (6, 3)], [(7, 4)]]
    make_inputs(0, 2)
    for k in range(1, 5):
        for j in range(3):
            for direction in range(2):
                landing(direction, k, j).wait_recv()
                if k < 4:
                    ring(direction, k + 1, j).start()
                    index, step = groups[k][direction]
                    to_sibling(index, at_z(step), j).start()
            if k == 4:
                index, step = groups[k][0]
                to_sibling(index, at_z(step), j).start()
            if k == 1:
                make_inputs(2 + 2 * j, 2)
        if k == 3:
            wr_begin()
        if k == 4:
            wr_step(1)
        for index, step in groups[k - 1]:
            multiply(index, at_z(step))
    for index, step in groups[4]:
        multiply(index, at_z(step))

    my_part = pl.ds(z * TOK, TOK)

    def unit_remote(u):
        return remote(
            units.at[u], ub.at[:, core, my_part], s_a.at[u], r_a.at[z], {"z": owner_of(u)}
        )

    def unit_local(u):
        return pltpu.make_async_copy(units.at[u], ub.at[:, core, my_part], r_a.at[z])

    for u in range(UNITS):
        p, h = u // 3, u % 3
        for j in range(3):
            units[u, j] = acc[j, p * TOK : (p + 1) * TOK, h * HD : (h + 1) * HD].astype(BF16)

        @pl.when(z == owner_of(u))
        def _(u=u):
            unit_local(u).start()

        @pl.when(z != owner_of(u))
        def _(u=u):
            unit_remote(u).start()

    wr_step(2)
    is_owner = lax.rem(z, 4) != 3
    mine = jnp.minimum(z - z // 4, UNITS - 1)
    mine_rows = pl.ds(pl.multiple_of((mine // 3) * TOK, TOK), TOK)
    mine_cols = pl.ds(pl.multiple_of(lax.rem(mine, 3) * HD, HD), HD)

    def arrived(source):
        block = ub.at[:, core, pl.ds(source * TOK, TOK)]
        return remote(block, block, s_a.at[0], r_a.at[source], sibling)

    def kv_to_sibling(source, which):
        block = ub.at[pl.ds(1, 2), which, pl.ds(source * TOK, TOK)]
        return remote(block, block, s_kv.at[source], r_kv.at[source], sibling)

    def o_remote(to):
        return remote(ob.at[to], att.at[f, mine_rows, mine_cols], s_o.at[to], r_o.at[mine], {"z": to})

    def o_local(to):
        return pltpu.make_async_copy(ob.at[to], att.at[f, mine_rows, mine_cols], r_o.at[mine])

    @pl.when(is_owner)
    def _():
        @pl.loop(0, NZ)
        def _(i):
            source = at_z(distance(i))
            arrived(source).wait_recv()
            kv_to_sibling(source, core).start()

        @pl.loop(0, NZ)
        def _(i):
            kv_to_sibling(at_z(distance(i)), 1 - core).wait_recv()


    wr_step(3)

    @pl.loop(0, NZ)
    def _(i):
        to = at_z(distance(NZ - 1 - i))

        @pl.when(is_owner)
        def _():
            queries = ub[0, core, pl.ds(pl.multiple_of(to * TOK, TOK), TOK), :]
            keys = ub[1].reshape(2 * NZ * TOK, HD)
            scores = lax.dot_general(
                queries, keys, (((1,), (1,)), ((), ())), preferred_element_type=F32
            )
            peak = jnp.max(scores, axis=1, keepdims=True)
            weight = jnp.exp2((scores - peak) * (HD**-0.5 * LOG2E))
            mass = jnp.sum(weight, axis=1, keepdims=True)
            result = jnp.dot(
                weight.astype(BF16), ub[2].reshape(2 * NZ * TOK, HD), preferred_element_type=F32
            )
            ob[to] = (result / mass).astype(BF16)

            @pl.when(to == z)
            def _():
                o_local(to).start()

            @pl.when(to != z)
            def _():
                o_remote(to).start()

        pl.when(i == 3)(functools.partial(wr_step, 4))

    other_f = (1 - y_lo) * 4 + x
    far_f = y_lo * 4 + lax.rem(x + 2, 4)
    x_up, x_down, x_far = ({"x": lax.rem(x + step, 4)} for step in (1, 3, 2))
    y_other = {"y_lo": 1 - y_lo}

    def att_copy(lane, source, p, device):
        block = att.at[source, pl.ds(p * TOK, TOK)]
        return remote(block, block, s_att.at[lane, p], r_att.at[source, p], device)

    def att_wait(source, p):
        att_copy(0, source, p, sibling).wait_recv()

    def att_first(p):
        return [
            att_copy(lane, f, p, device) for lane, device in enumerate((x_up, x_down, y_other, x_far))
        ]

    def att_second(p):
        return [att_copy(4, other_f, p, x_up), att_copy(5, other_f, p, x_down)]

    def att_third(p):
        return [att_copy(6, far_f, p, y_other)]

    def first(p):
        for h in range(3):
            block = att.at[f, pl.ds(p * TOK, TOK), pl.ds(h * HD, HD)]
            remote(block, block, s_o.at[0], r_o.at[p * 3 + h], sibling).wait_recv()
        for copy in att_first(p):
            copy.start()

    def second(p):
        att_wait(other_f, p)
        for copy in att_second(p):
            copy.start()

    def third(p):
        att_wait(far_f, p)
        for copy in att_third(p):
            copy.start()

    first(0)
    first(1)
    target_load.wait()
    difference = target[...].astype(F32) - lat[:, window].astype(F32)

    @pl.when(lax.rem(out_block, 2) == 0)
    def _():
        base[...] = difference[:, :ROWS]

    @pl.when(lax.rem(out_block, 2) == 1)
    def _():
        base[...] = difference[:, COLS - ROWS :]

    second(0)
    third(0)

    @pl.loop(0, 8)
    def _(source):
        wo_forward(source)

    second(1)
    third(1)

    def fin_copy(half, p):
        return remote(
            pb.at[half, p], fin.at[y_hi, p], s_f.at[half, p], r_f.at[y_hi, p], {"core": half, "y_hi": core}
        )

    def send_half(half, p):
        stays = (core == half) & (y_hi == core)

        @pl.when(stays)
        def _():
            pltpu.make_async_copy(pb.at[half, p], fin.at[y_hi, p], r_f.at[y_hi, p]).start()

        @pl.when(jnp.logical_not(stays))
        def _():
            fin_copy(half, p).start()

    near = [y_lo * 4 + lax.rem(x + step, 4) for step in (1, 3)]
    across = [(1 - y_lo) * 4 + lax.rem(x + step, 4) for step in (1, 3, 2)]
    for p in range(2):
        rows = pl.ds(p * TOK, TOK)
        for place, source in enumerate([f, other_f, far_f, *near, *across]):
            if place > 2:
                att_wait(source, p)
            if p == 0:
                block = wo.at[1 - core, source]
                remote(block, block, s_ws.at[source], r_wo.at[1 - core, source], sibling).wait_recv()
            for half in range(2):
                product = lax.dot_general(
                    att[source, rows], wo[half, source], (((1,), (1,)), ((), ())), preferred_element_type=F32
                )
                if place == 0:
                    pred[half] = product
                elif place < 7:
                    pred[half] += product
                else:
                    pb[half, p] = (pred[half] + product).astype(BF16)
                    send_half(half, p)

    for p in range(2):
        for section in range(2):
            block = fin.at[section, p]
            remote(block, block, s_f.at[0, p], r_f.at[section, p], sibling).wait_recv()

    def found(section, p):
        return fin[section, p].astype(F32)

    dmd[...] = found(1, 0) - (found(0, 1) + GUIDANCE * (found(0, 0) - found(0, 1)))
    residual[...] = found(1, 1) - base[...]

    @pl.when(swapped)
    def _():
        for j in range(3):
            own_remote(j).wait_send()
        wr_own_remote().wait_send()
        for slot in range(NZ):
            h_copy(slot).wait_send()

    for slot in range(NZ):
        wr_out(slot, "wait")
        wo_share(slot).wait_send()
    for k in range(1, 5):
        for direction in range(2):
            wr_copy(direction, k, 0).wait_send()
    for k in range(1, 5):
        for j in range(3):
            for direction in range(2):
                ring(direction, k, j).wait_send()
    for group in groups:
        for index, step in group:
            for j in range(3):
                to_sibling(index, at_z(step), j).wait_send()
    for u in range(UNITS):

        @pl.when(z != owner_of(u))
        def _(u=u):
            unit_remote(u).wait_send()

    @pl.when(is_owner)
    def _():
        for source in range(NZ):
            kv_to_sibling(source, core).wait_send()

            @pl.when(z != source)
            def _(source=source):
                o_remote(source).wait_send()

    for p in range(2):
        for copy in att_first(p) + att_second(p) + att_third(p):
            copy.wait_send()
    for half in range(2):

        @pl.when(jnp.logical_not((core == half) & (y_hi == core)))
        def _(half=half):
            for p in range(2):
                fin_copy(half, p).wait_send()


def outputs(times, pair, latents, noise, cond_table, gain, w_qkv, w_out):
    dma = pltpu.SemaphoreType.DMA
    vmem, any_space = pl.BlockSpec(memory_space=pltpu.VMEM), pl.BlockSpec(memory_space=pl.ANY)
    smem = pl.BlockSpec(memory_space=pltpu.SMEM)
    return pl.pallas_call(
        step_kernel,
        out_shape=[jax.ShapeDtypeStruct((TOK, ROWS), F32)] * 2,
        in_specs=[smem, smem, any_space, any_space, vmem, vmem, any_space, any_space],
        out_specs=[vmem, vmem],
        scratch_shapes=[
            pltpu.VMEM((TOK, NZ * DZ), BF16),
            pltpu.VMEM((2, TOK, NZ * DZ), BF16),
            pltpu.VMEM((2, NZ * DZ), F32),
            pltpu.VMEM((2, NZ, 2 * TOK, DZ), BF16),
            pltpu.VMEM((2, TOK, 1), F32),
            pltpu.VMEM((NZ, 3, DZ, COLS), BF16),
            pltpu.VMEM((3, 2 * TOK, COLS), F32),
            pltpu.VMEM((UNITS, 3, TOK, HD), BF16),
            pltpu.VMEM((3, 2, NZ * TOK, HD), BF16),
            pltpu.VMEM((NZ, TOK, HD), BF16),
            pltpu.VMEM((8, 2 * TOK, COLS), BF16),
            pltpu.VMEM((NZ, ROWS, COLS), BF16),
            pltpu.VMEM((2, 8, ROWS, COLS), BF16),
            pltpu.VMEM((2, TOK, ROWS), F32),
            pltpu.VMEM((2, 2, TOK, ROWS), BF16),
            pltpu.VMEM((2, 2, TOK, ROWS), BF16),
            pltpu.VMEM((TOK, COLS), BF16),
            pltpu.VMEM((TOK, ROWS), F32),
            dma((4,)),
            dma((3,)), dma((3,)),
            dma((NZ,)), dma((NZ,)),
            dma((2, 4, 3)), dma((2, 4, 3)),
            dma((NZ, 3)), dma((NZ, 3)),
            dma((UNITS,)), dma((NZ,)),
            dma((NZ,)), dma((NZ,)),
            dma((NZ,)), dma((UNITS,)),
            dma((2, 5)), dma((2, 5)), dma((NZ,)), dma((2, 8)), dma((8,)),
            dma((7, 2)), dma((8, 2)),
            dma((2, 2)), dma((2, 2)),
        ],
        compiler_params=pltpu.CompilerParams(
            collective_id=0, has_side_effects=True, vmem_limit_bytes=60 * 2**20
        ),
        cost_estimate=pl.CostEstimate(
            flops=9_000_000_000, bytes_accessed=40_000_000, transcendentals=5_000_000
        ),
    )(times, pair, latents, noise, cond_table, gain, w_qkv, w_out)


def body(latents, noise, time_index, cfg_pair, cond_table, gain, w_qkv, w_out):
    return tuple(
        outputs(
            time_index, cfg_pair, latents, noise, cond_table, gain, w_qkv, jnp.swapaxes(w_out[0], 0, 1)
        )
    )


def solution(mesh):
    torus = Mesh(mesh.devices.reshape(2, NZ, 2, 2, 4), AXES)
    seq, fsdp = ("z", "y_hi"), ("y_lo", "x")
    return jax.shard_map(
        body,
        mesh=torus,
        in_specs=(
            P(seq, None),
            P(None, seq, None),
            P(),
            P(),
            P(),
            P("core", None),
            P("core", None, seq, fsdp),
            P("core", fsdp, seq),
        ),
        out_specs=(P(seq, ("core", *fsdp)), P(seq, ("core", *fsdp))),
        check_vma=False,
    )
```

```python
import functools

import jax
import jax.numpy as jnp
from jax import lax
from jax.experimental import pallas as pl
from jax.experimental.pallas import tpu as pltpu
from jax.sharding import Mesh
from jax.sharding import PartitionSpec as P

HD = 128
LOG2E = 1.4426950408889634
GUIDANCE = 3.5
EPSILON = 1e-06
MESH = pl.DeviceIdType.MESH
BF16, F32 = jnp.bfloat16, jnp.float32

AXES = ("core", "z", "y_hi", "y_lo", "x")
NZ = 8
TOK = 192
DZ = 640
ROWS = 320
COLS = 384
UNITS = 6
RB = 64


def owner_of(unit):
    return unit + unit // 3


def step_kernel(
    times, pair, lat_hbm, noise_hbm, cond, gain, w_hbm, wo_hbm, dmd, residual,
    lat, noi, shift, hb, inv, wbuf, acc, units, ub, ob, att, wr, wo, pred, pb, fin, target, base,
    s_in, s_w, r_w, s_h, r_h, s_ring, r_ring, s_sib, r_sib, s_a, r_a, s_kv, r_kv, s_o, r_o,
    s_wr, r_wr, s_wo, r_wo, s_ws, s_att, r_att, s_far, r_far, s_f, r_f,
):
    core, z, y_hi = lax.axis_index("core"), lax.axis_index("z"), lax.axis_index("y_hi")
    y_lo, x = lax.axis_index("y_lo"), lax.axis_index("x")
    f = y_lo * 4 + x
    swapped = core != y_hi
    sel = lax.rem(core + y_hi, 2)
    partner = {"core": 1 - core, "y_hi": 1 - y_hi}
    sibling = {"core": 1 - core}

    def at_z(step):
        return lax.rem(z + step + NZ, NZ)

    def at_f(step):
        return lax.rem(f + step, 8)

    def f_device(peer):
        return {"y_lo": peer // 4, "x": lax.rem(peer, 4)}

    def remote(src, dst, send, recv, device):
        return pltpu.make_async_remote_copy(
            src_ref=src, dst_ref=dst, send_sem=send, recv_sem=recv, device_id=device, device_id_type=MESH
        )

    loads = [
        pltpu.make_async_copy(lat_hbm, lat, s_in.at[0]),
        pltpu.make_async_copy(noise_hbm.at[0], noi.at[0], s_in.at[1]),
        pltpu.make_async_copy(noise_hbm.at[core], noi.at[1], s_in.at[2]),
    ]
    out_block = core * 8 + f
    window = pl.ds(pl.multiple_of(((out_block * 5) // 2) * 128, 128), COLS)
    target_load = pltpu.make_async_copy(noise_hbm.at[1, :, window], target, s_in.at[3])
    target_load.start()
    for load in loads:
        load.start()

    my_rows = pl.ds(core * ROWS, ROWS)
    sib_rows = pl.ds((1 - core) * ROWS, ROWS)

    def own_local(j):
        return pltpu.make_async_copy(w_hbm.at[0, j], wbuf.at[z, j, my_rows], r_w.at[j])

    def wr_own_local():
        return pltpu.make_async_copy(wo_hbm, wr.at[z], r_wr.at[0, 0])

    @pl.when(jnp.logical_not(swapped))
    def _():
        for j in range(3):
            own_local(j).start()
        wr_own_local().start()

    barrier = pltpu.get_barrier_semaphore()

    def greet(device):
        pl.semaphore_signal(barrier, inc=1, device_id=device, device_id_type=MESH)

    greet(partner)
    greet(sibling)
    greet({"y_hi": 1 - y_hi})
    for step in range(1, NZ):
        greet({"z": at_z(step)})
    for step in range(1, 8):
        greet(f_device(at_f(step)))
    same = lax.rem(x, 2) == core

    @pl.when(jnp.logical_not(same))
    def _():
        for step in range(1, 8):
            greet({"core": 1 - core, **f_device(at_f(step))})

    @pl.when(same)
    def _():
        pl.semaphore_wait(barrier, 20)

    @pl.when(jnp.logical_not(same))
    def _():
        pl.semaphore_wait(barrier, 21)

    def own_remote(j):
        return remote(
            w_hbm.at[0, j], wbuf.at[z, j, pl.ds(y_hi * ROWS, ROWS)], s_w.at[j], r_w.at[j], partner
        )

    def wr_own_remote():
        return remote(wo_hbm, wr.at[z], s_wr.at[0, 0], r_wr.at[0, 0], partner)

    @pl.when(swapped)
    def _():
        for j in range(3):
            own_remote(j).start()

    def ring_copy(direction, k, j, moved):
        sign = 1 - 2 * direction
        slot = at_z(-sign * (k - 1 + moved))
        if k < 4:
            rows = my_rows
        else:
            rows = pl.ds(core * ROWS + direction * (ROWS // 2), ROWS // 2)
        block = wbuf.at[slot, j, rows]
        return remote(
            block, block, s_ring.at[direction, k - 1, j], r_ring.at[direction, k - 1, j], {"z": at_z(sign)}
        )

    def ring(direction, k, j):
        return ring_copy(direction, k, j, 0)

    def landing(direction, k, j):
        return ring_copy(direction, k, j, 1)

    def to_sibling(index, slot, j):
        block = wbuf.at[slot, j, my_rows]
        return remote(block, block, s_sib.at[index, j], r_sib.at[index, j], sibling)

    def from_sibling(index, slot, j):
        block = wbuf.at[slot, j, sib_rows]
        return remote(block, block, s_sib.at[index, j], r_sib.at[index, j], sibling)

    def begin_ring():
        for j in range(3):
            own_local(j).wait()
            ring(0, 1, j).start()
            ring(1, 1, j).start()
            to_sibling(0, z, j).start()

    pl.when(jnp.logical_not(swapped))(begin_ring)

    def wr_copy(direction, k, moved):
        sign = 1 - 2 * direction
        slot = at_z(-sign * (k - 1 + moved))
        rows = pl.ds(0, ROWS) if k < 4 else pl.ds(direction * (ROWS // 2), ROWS // 2)
        block = wr.at[slot, rows]
        return remote(block, block, s_wr.at[direction, k], r_wr.at[direction, k], {"z": at_z(sign)})

    def wr_out(slot, act):
        half, to = slot // 4, 2 * lax.rem(slot, 4) + core
        here = (to == f) & (half == core)

        @pl.when(jnp.logical_not(here))
        def _():
            copy = remote(
                wr.at[slot], wo.at[half, f], s_wo.at[slot], r_wo.at[half, f],
                {"core": half, **f_device(to)},
            )
            if act == "send":
                copy.start()
            else:
                copy.wait_send()

        if act == "send":

            @pl.when(here)
            def _():
                pltpu.make_async_copy(wr.at[slot], wo.at[half, f], r_wo.at[half, f]).start()

    def wr_begin():
        wr_own_local().wait()
        wr_copy(0, 1, 0).start()
        wr_copy(1, 1, 0).start()
        wr_out(z, "send")

    def wr_step(k):
        for direction in range(2):
            wr_copy(direction, k, 1).wait_recv()
            if k < 4:
                wr_copy(direction, k + 1, 0).start()
                wr_out(at_z((2 * direction - 1) * k), "send")
        if k == 4:
            wr_out(at_z(4), "send")

    def wo_share(source):
        block = wo.at[core, source]
        return remote(block, block, s_ws.at[source], r_wo.at[core, source], sibling)

    def wo_forward(source):
        wo_share(source).wait_recv()
        wo_share(source).start()

    def level_of(step_index):
        fraction = jnp.full((8, 128), step_index.astype(F32)) / 1000.0
        return (5.0 * fraction / (1.0 + 4.0 * fraction))[0:1, 0:1]

    levels = (level_of(times[0]), level_of(times[core]))
    shift[0:1, :] = cond[pl.ds(pair[0], 1), :]
    shift[1:2, :] = cond[pl.ds(pair[1 - core], 1), :]
    for load in loads:
        load.wait()

    def mixed(p, rows, cols):
        return (1.0 - levels[p]) * lat[rows, cols].astype(F32) + levels[p] * noi[p, rows, cols].astype(F32)

    for p in range(2):

        @pl.loop(0, TOK // 16)
        def _(b, p=p):
            rows = pl.ds(pl.multiple_of(b * 16, 16), 16)
            total = jnp.zeros((16, DZ), F32)
            for q in range(NZ):
                part = mixed(p, rows, pl.ds(q * DZ, DZ))
                total = total + part * part
            mean = jnp.sum(total, axis=1, keepdims=True) * (1.0 / (NZ * DZ))
            inv[p, rows, :] = lax.rsqrt(mean + EPSILON)

    pl.when(swapped)(begin_ring)

    @pl.when(swapped)
    def _():
        wr_own_remote().start()

    def h_copy(slot):
        return remote(hb.at[0, slot], hb.at[1, slot], s_h.at[slot], r_h.at[slot], partner)

    def distance(i):
        return lax.rem(i + 1, 2) * (-((i + 1) // 2)) + lax.rem(i, 2) * ((i + 1) // 2)

    def make_inputs(first, count):
        @pl.loop(first, first + count)
        def _(i):
            slot = at_z(distance(i))
            cols = pl.ds(pl.multiple_of(slot * DZ, 128), DZ)
            for p in range(2):

                @pl.loop(0, TOK // RB)
                def _(b, p=p):
                    start = pl.multiple_of(b * RB, RB)
                    rows = pl.ds(start, RB)
                    part = mixed(p, rows, cols) * inv[p, rows, :] * gain[:, cols] + shift[p : p + 1, cols]
                    hb[0, slot, pl.ds(p * TOK + start, RB), :] = part.astype(BF16)

            @pl.when(swapped)
            def _():
                h_copy(slot).start()

    acc[...] = jnp.zeros_like(acc)

    def multiply(index, slot):
        for j in range(3):
            from_sibling(index, slot, j).wait_recv()

        @pl.when(swapped)
        def _():
            h_copy(slot).wait_recv()

        @pl.loop(0, 3)
        def _(j):
            acc[j] += jnp.dot(hb[sel, slot], wbuf[slot, j], preferred_element_type=F32)

    groups = [[(0, 0)], [(1, -1), (2, 1)], [(3, -2), (4, 2)], [(5, -3), (6, 3)], [(7, 4)]]
    make_inputs(0, 2)
    for k in range(1, 5):
        if k == 4:
            for index, step in groups[3]:
                multiply(index, at_z(step))
        for j in range(3):
            for direction in range(2):
                landing(direction, k, j).wait_recv()
                if k < 4:
                    ring(direction, k + 1, j).start()
                    index, step = groups[k][direction]
                    to_sibling(index, at_z(step), j).start()
            if k == 4:
                index, step = groups[k][0]
                to_sibling(index, at_z(step), j).start()
            if k == 1:
                make_inputs(2 + 2 * j, 2)
        if k == 3:
            wr_begin()
        if k == 4:
            wr_step(1)
        if k < 4:
            for index, step in groups[k - 1]:
                multiply(index, at_z(step))
    for index, step in groups[4]:
        multiply(index, at_z(step))

    my_part = pl.ds(z * TOK, TOK)

    def unit_remote(u):
        return remote(
            units.at[u], ub.at[:, core, my_part], s_a.at[u], r_a.at[z], {"z": owner_of(u)}
        )

    def unit_local(u):
        return pltpu.make_async_copy(units.at[u], ub.at[:, core, my_part], r_a.at[z])

    for u in range(UNITS):
        p, h = u // 3, u % 3
        for j in range(3):
            units[u, j] = acc[j, p * TOK : (p + 1) * TOK, h * HD : (h + 1) * HD].astype(BF16)

        @pl.when(z == owner_of(u))
        def _(u=u):
            unit_local(u).start()

        @pl.when(z != owner_of(u))
        def _(u=u):
            unit_remote(u).start()

    wr_step(2)
    is_owner = lax.rem(z, 4) != 3
    mine = jnp.minimum(z - z // 4, UNITS - 1)
    mine_rows = pl.ds(pl.multiple_of((mine // 3) * TOK, TOK), TOK)
    mine_cols = pl.ds(pl.multiple_of(lax.rem(mine, 3) * HD, HD), HD)

    def arrived(source):
        block = ub.at[:, core, pl.ds(source * TOK, TOK)]
        return remote(block, block, s_a.at[0], r_a.at[source], sibling)

    def kv_to_sibling(source, which):
        block = ub.at[pl.ds(1, 2), which, pl.ds(source * TOK, TOK)]
        return remote(block, block, s_kv.at[source], r_kv.at[source], sibling)

    def o_remote(to):
        return remote(ob.at[to], att.at[f, mine_rows, mine_cols], s_o.at[to], r_o.at[mine], {"z": to})

    def o_local(to):
        return pltpu.make_async_copy(ob.at[to], att.at[f, mine_rows, mine_cols], r_o.at[mine])

    @pl.when(is_owner)
    def _():
        @pl.loop(0, NZ)
        def _(i):
            source = at_z(distance(i))
            arrived(source).wait_recv()
            kv_to_sibling(source, core).start()

        @pl.loop(0, NZ)
        def _(i):
            kv_to_sibling(at_z(distance(i)), 1 - core).wait_recv()


    wr_step(3)

    @pl.loop(0, NZ)
    def _(i):
        to = at_z(distance(NZ - 1 - i))

        @pl.when(is_owner)
        def _():
            queries = ub[0, core, pl.ds(pl.multiple_of(to * TOK, TOK), TOK), :]
            keys = ub[1].reshape(2 * NZ * TOK, HD)
            scores = lax.dot_general(
                queries, keys, (((1,), (1,)), ((), ())), preferred_element_type=F32
            )
            peak = jnp.max(scores, axis=1, keepdims=True)
            weight = jnp.exp2((scores - peak) * (HD**-0.5 * LOG2E))
            mass = jnp.sum(weight, axis=1, keepdims=True)
            result = jnp.dot(
                weight.astype(BF16), ub[2].reshape(2 * NZ * TOK, HD), preferred_element_type=F32
            )
            ob[to] = (result / mass).astype(BF16)

            @pl.when(to == z)
            def _():
                o_local(to).start()

            @pl.when(to != z)
            def _():
                o_remote(to).start()

        pl.when(i == 3)(functools.partial(wr_step, 4))

    other_f = (1 - y_lo) * 4 + x
    far_f = y_lo * 4 + lax.rem(x + 2, 4)
    x_up, x_down = ({"x": lax.rem(x + step, 4)} for step in (1, 3))
    left_f, right_f = (y_lo * 4 + lax.rem(x + step, 4) for step in (3, 1))
    y_other = {"y_lo": 1 - y_lo}

    def att_copy(lane, source, p, device):
        block = att.at[source, pl.ds(p * TOK, TOK)]
        return remote(block, block, s_att.at[lane, p], r_att.at[source, p], device)

    def att_wait(source, p):
        att_copy(0, source, p, sibling).wait_recv()

    def att_first(p):
        return [
            att_copy(lane, f, p, device) for lane, device in enumerate((x_up, x_down, y_other))
        ]

    def far_half(lane, source, p):
        block = att.at[source, pl.ds(p * TOK + lane * (TOK // 2), TOK // 2)]
        return remote(block, block, s_far.at[lane, p], r_far.at[lane, p], (x_up, x_down)[lane])

    def pass_on(p):
        for lane, source in ((0, left_f), (1, right_f)):
            att_wait(source, p)
            far_half(lane, source, p).start()

    def att_second(p):
        return [att_copy(4, other_f, p, x_up), att_copy(5, other_f, p, x_down)]

    def att_third(p):
        return [att_copy(6, far_f, p, y_other)]

    def first(p):
        for h in range(3):
            block = att.at[f, pl.ds(p * TOK, TOK), pl.ds(h * HD, HD)]
            remote(block, block, s_o.at[0], r_o.at[p * 3 + h], sibling).wait_recv()
        for copy in att_first(p):
            copy.start()

    def second(p):
        att_wait(other_f, p)
        for copy in att_second(p):
            copy.start()

    def third(p):
        for lane in range(2):
            far_half(lane, far_f, p).wait_recv()
        for copy in att_third(p):
            copy.start()

    first(0)
    first(1)
    target_load.wait()
    difference = target[...].astype(F32) - lat[:, window].astype(F32)

    @pl.when(lax.rem(out_block, 2) == 0)
    def _():
        base[...] = difference[:, :ROWS]

    @pl.when(lax.rem(out_block, 2) == 1)
    def _():
        base[...] = difference[:, COLS - ROWS :]

    pass_on(0)
    second(0)
    third(0)

    @pl.loop(0, 8)
    def _(source):
        wo_forward(source)

    pass_on(1)
    second(1)
    third(1)

    def fin_copy(half, p):
        return remote(
            pb.at[half, p], fin.at[y_hi, p], s_f.at[half, p], r_f.at[y_hi, p], {"core": half, "y_hi": core}
        )

    def send_half(half, p):
        stays = (core == half) & (y_hi == core)

        @pl.when(stays)
        def _():
            pltpu.make_async_copy(pb.at[half, p], fin.at[y_hi, p], r_f.at[y_hi, p]).start()

        @pl.when(jnp.logical_not(stays))
        def _():
            fin_copy(half, p).start()

    near = [y_lo * 4 + lax.rem(x + step, 4) for step in (1, 3)]
    across = [(1 - y_lo) * 4 + lax.rem(x + step, 4) for step in (1, 3, 2)]
    for p in range(2):
        rows = pl.ds(p * TOK, TOK)
        for place, source in enumerate([f, other_f, far_f, *near, *across]):
            if place > 4:
                att_wait(source, p)
            if p == 0:
                block = wo.at[1 - core, source]
                remote(block, block, s_ws.at[source], r_wo.at[1 - core, source], sibling).wait_recv()
            for half in range(2):
                product = lax.dot_general(
                    att[source, rows], wo[half, source], (((1,), (1,)), ((), ())), preferred_element_type=F32
                )
                if place == 0:
                    pred[half] = product
                elif place < 7:
                    pred[half] += product
                else:
                    pb[half, p] = (pred[half] + product).astype(BF16)
                    send_half(half, p)

    for p in range(2):
        for section in range(2):
            block = fin.at[section, p]
            remote(block, block, s_f.at[0, p], r_f.at[section, p], sibling).wait_recv()

    def found(section, p):
        return fin[section, p].astype(F32)

    dmd[...] = found(1, 0) - (found(0, 1) + GUIDANCE * (found(0, 0) - found(0, 1)))
    residual[...] = found(1, 1) - base[...]

    @pl.when(swapped)
    def _():
        for j in range(3):
            own_remote(j).wait_send()
        wr_own_remote().wait_send()
        for slot in range(NZ):
            h_copy(slot).wait_send()

    for slot in range(NZ):
        wr_out(slot, "wait")
        wo_share(slot).wait_send()
    for k in range(1, 5):
        for direction in range(2):
            wr_copy(direction, k, 0).wait_send()
    for k in range(1, 5):
        for j in range(3):
            for direction in range(2):
                ring(direction, k, j).wait_send()
    for group in groups:
        for index, step in group:
            for j in range(3):
                to_sibling(index, at_z(step), j).wait_send()
    for u in range(UNITS):

        @pl.when(z != owner_of(u))
        def _(u=u):
            unit_remote(u).wait_send()

    @pl.when(is_owner)
    def _():
        for source in range(NZ):
            kv_to_sibling(source, core).wait_send()

            @pl.when(z != source)
            def _(source=source):
                o_remote(source).wait_send()

    for p in range(2):
        far_half(0, left_f, p).wait_send()
        far_half(1, right_f, p).wait_send()
        for copy in att_first(p) + att_second(p) + att_third(p):
            copy.wait_send()
    for half in range(2):

        @pl.when(jnp.logical_not((core == half) & (y_hi == core)))
        def _(half=half):
            for p in range(2):
                fin_copy(half, p).wait_send()


def outputs(times, pair, latents, noise, cond_table, gain, w_qkv, w_out):
    dma = pltpu.SemaphoreType.DMA
    vmem, any_space = pl.BlockSpec(memory_space=pltpu.VMEM), pl.BlockSpec(memory_space=pl.ANY)
    smem = pl.BlockSpec(memory_space=pltpu.SMEM)
    return pl.pallas_call(
        step_kernel,
        out_shape=[jax.ShapeDtypeStruct((TOK, ROWS), F32)] * 2,
        in_specs=[smem, smem, any_space, any_space, vmem, vmem, any_space, any_space],
        out_specs=[vmem, vmem],
        scratch_shapes=[
            pltpu.VMEM((TOK, NZ * DZ), BF16),
            pltpu.VMEM((2, TOK, NZ * DZ), BF16),
            pltpu.VMEM((2, NZ * DZ), F32),
            pltpu.VMEM((2, NZ, 2 * TOK, DZ), BF16),
            pltpu.VMEM((2, TOK, 1), F32),
            pltpu.VMEM((NZ, 3, DZ, COLS), BF16),
            pltpu.VMEM((3, 2 * TOK, COLS), F32),
            pltpu.VMEM((UNITS, 3, TOK, HD), BF16),
            pltpu.VMEM((3, 2, NZ * TOK, HD), BF16),
            pltpu.VMEM((NZ, TOK, HD), BF16),
            pltpu.VMEM((8, 2 * TOK, COLS), BF16),
            pltpu.VMEM((NZ, ROWS, COLS), BF16),
            pltpu.VMEM((2, 8, ROWS, COLS), BF16),
            pltpu.VMEM((2, TOK, ROWS), F32),
            pltpu.VMEM((2, 2, TOK, ROWS), BF16),
            pltpu.VMEM((2, 2, TOK, ROWS), BF16),
            pltpu.VMEM((TOK, COLS), BF16),
            pltpu.VMEM((TOK, ROWS), F32),
            dma((4,)),
            dma((3,)), dma((3,)),
            dma((NZ,)), dma((NZ,)),
            dma((2, 4, 3)), dma((2, 4, 3)),
            dma((NZ, 3)), dma((NZ, 3)),
            dma((UNITS,)), dma((NZ,)),
            dma((NZ,)), dma((NZ,)),
            dma((NZ,)), dma((UNITS,)),
            dma((2, 5)), dma((2, 5)), dma((NZ,)), dma((2, 8)), dma((8,)),
            dma((7, 2)), dma((8, 2)),
            dma((2, 2)), dma((2, 2)),
            dma((2, 2)), dma((2, 2)),
        ],
        compiler_params=pltpu.CompilerParams(
            collective_id=0, has_side_effects=True, vmem_limit_bytes=60 * 2**20
        ),
        cost_estimate=pl.CostEstimate(
            flops=9_000_000_000, bytes_accessed=40_000_000, transcendentals=5_000_000
        ),
    )(times, pair, latents, noise, cond_table, gain, w_qkv, w_out)


def body(latents, noise, time_index, cfg_pair, cond_table, gain, w_qkv, w_out):
    return tuple(
        outputs(
            time_index, cfg_pair, latents, noise, cond_table, gain, w_qkv, jnp.swapaxes(w_out[0], 0, 1)
        )
    )


def solution(mesh):
    torus = Mesh(mesh.devices.reshape(2, NZ, 2, 2, 4), AXES)
    seq, fsdp = ("z", "y_hi"), ("y_lo", "x")
    return jax.shard_map(
        body,
        mesh=torus,
        in_specs=(
            P(seq, None),
            P(None, seq, None),
            P(),
            P(),
            P(),
            P("core", None),
            P("core", None, seq, fsdp),
            P("core", fsdp, seq),
        ),
        out_specs=(P(seq, ("core", *fsdp)), P(seq, ("core", *fsdp))),
        check_vma=False,
    )
```

```python
import functools

import jax
import jax.numpy as jnp
from jax import lax
from jax.experimental import pallas as pl
from jax.experimental.pallas import tpu as pltpu
from jax.sharding import Mesh
from jax.sharding import PartitionSpec as P

HD = 128
LOG2E = 1.4426950408889634
GUIDANCE = 3.5
EPSILON = 1e-06
MESH = pl.DeviceIdType.MESH
BF16, F32 = jnp.bfloat16, jnp.float32

AXES = ("core", "z", "y_hi", "y_lo", "x")
NZ = 8
TOK = 192
DZ = 640
ROWS = 320
COLS = 384
UNITS = 6
RB = 64


def owner_of(unit):
    return unit + unit // 3


def step_kernel(
    times, pair, lat_hbm, noise_hbm, cond, gain, w_hbm, wo_hbm, dmd, residual,
    lat, noi, shift, hb, inv, wbuf, acc, units, ub, ob, att, wr, wo, pred, pb, fin, target, base,
    s_in, s_w, r_w, s_h, r_h, s_ring, r_ring, s_sib, r_sib, s_a, r_a, s_kv, r_kv, s_o, r_o,
    s_wr, r_wr, s_wo, r_wo, s_ws, s_att, r_att, s_far, r_far, s_f, r_f,
):
    core, z, y_hi = lax.axis_index("core"), lax.axis_index("z"), lax.axis_index("y_hi")
    y_lo, x = lax.axis_index("y_lo"), lax.axis_index("x")
    f = y_lo * 4 + x
    swapped = core != y_hi
    sel = lax.rem(core + y_hi, 2)
    partner = {"core": 1 - core, "y_hi": 1 - y_hi}
    sibling = {"core": 1 - core}

    def at_z(step):
        return lax.rem(z + step + NZ, NZ)

    def at_f(step):
        return lax.rem(f + step, 8)

    def f_device(peer):
        return {"y_lo": peer // 4, "x": lax.rem(peer, 4)}

    def remote(src, dst, send, recv, device):
        return pltpu.make_async_remote_copy(
            src_ref=src, dst_ref=dst, send_sem=send, recv_sem=recv, device_id=device, device_id_type=MESH
        )

    loads = [
        pltpu.make_async_copy(lat_hbm, lat, s_in.at[0]),
        pltpu.make_async_copy(noise_hbm.at[0], noi.at[0], s_in.at[1]),
        pltpu.make_async_copy(noise_hbm.at[core], noi.at[1], s_in.at[2]),
    ]
    out_block = core * 8 + f
    window = pl.ds(pl.multiple_of(((out_block * 5) // 2) * 128, 128), COLS)
    target_load = pltpu.make_async_copy(noise_hbm.at[1, :, window], target, s_in.at[3])
    target_load.start()
    for load in loads:
        load.start()

    my_rows = pl.ds(core * ROWS, ROWS)
    sib_rows = pl.ds((1 - core) * ROWS, ROWS)

    def own_local(j):
        return pltpu.make_async_copy(w_hbm.at[0, j], wbuf.at[z, j, my_rows], r_w.at[j])

    def wr_own_local():
        return pltpu.make_async_copy(wo_hbm, wr.at[z], r_wr.at[0, 0])

    @pl.when(jnp.logical_not(swapped))
    def _():
        for j in range(3):
            own_local(j).start()
        wr_own_local().start()

    barrier = pltpu.get_barrier_semaphore()

    def greet(device):
        pl.semaphore_signal(barrier, inc=1, device_id=device, device_id_type=MESH)

    greet(partner)
    greet(sibling)
    greet({"y_hi": 1 - y_hi})
    for step in range(1, NZ):
        greet({"z": at_z(step)})
    for step in range(1, 8):
        greet(f_device(at_f(step)))
    same = lax.rem(x, 2) == core

    @pl.when(jnp.logical_not(same))
    def _():
        for step in range(1, 8):
            greet({"core": 1 - core, **f_device(at_f(step))})

    @pl.when(same)
    def _():
        pl.semaphore_wait(barrier, 20)

    @pl.when(jnp.logical_not(same))
    def _():
        pl.semaphore_wait(barrier, 21)

    def own_remote(j):
        return remote(
            w_hbm.at[0, j], wbuf.at[z, j, pl.ds(y_hi * ROWS, ROWS)], s_w.at[j], r_w.at[j], partner
        )

    def wr_own_remote():
        return remote(wo_hbm, wr.at[z], s_wr.at[0, 0], r_wr.at[0, 0], partner)

    @pl.when(swapped)
    def _():
        for j in range(3):
            own_remote(j).start()

    def ring_copy(direction, k, j, moved):
        sign = 1 - 2 * direction
        slot = at_z(-sign * (k - 1 + moved))
        if k < 4:
            rows = my_rows
        else:
            rows = pl.ds(core * ROWS + direction * (ROWS // 2), ROWS // 2)
        block = wbuf.at[slot, j, rows]
        return remote(
            block, block, s_ring.at[direction, k - 1, j], r_ring.at[direction, k - 1, j], {"z": at_z(sign)}
        )

    def ring(direction, k, j):
        return ring_copy(direction, k, j, 0)

    def landing(direction, k, j):
        return ring_copy(direction, k, j, 1)

    def to_sibling(index, slot, j):
        block = wbuf.at[slot, j, my_rows]
        return remote(block, block, s_sib.at[index, j], r_sib.at[index, j], sibling)

    def from_sibling(index, slot, j):
        block = wbuf.at[slot, j, sib_rows]
        return remote(block, block, s_sib.at[index, j], r_sib.at[index, j], sibling)

    def begin_ring():
        for j in range(3):
            own_local(j).wait()
            ring(0, 1, j).start()
            ring(1, 1, j).start()
            to_sibling(0, z, j).start()

    pl.when(jnp.logical_not(swapped))(begin_ring)

    def wr_copy(direction, k, moved):
        sign = 1 - 2 * direction
        slot = at_z(-sign * (k - 1 + moved))
        rows = pl.ds(0, ROWS) if k < 4 else pl.ds(direction * (ROWS // 2), ROWS // 2)
        block = wr.at[slot, rows]
        return remote(block, block, s_wr.at[direction, k], r_wr.at[direction, k], {"z": at_z(sign)})

    def wr_out(slot, act):
        half, to = slot // 4, 2 * lax.rem(slot, 4) + core
        here = (to == f) & (half == core)

        @pl.when(jnp.logical_not(here))
        def _():
            copy = remote(
                wr.at[slot], wo.at[half, f], s_wo.at[slot], r_wo.at[half, f],
                {"core": half, **f_device(to)},
            )
            if act == "send":
                copy.start()
            else:
                copy.wait_send()

        if act == "send":

            @pl.when(here)
            def _():
                pltpu.make_async_copy(wr.at[slot], wo.at[half, f], r_wo.at[half, f]).start()

    def wr_begin():
        wr_own_local().wait()
        wr_copy(0, 1, 0).start()
        wr_copy(1, 1, 0).start()
        wr_out(z, "send")

    def wr_step(k):
        for direction in range(2):
            wr_copy(direction, k, 1).wait_recv()
            if k < 4:
                wr_copy(direction, k + 1, 0).start()
                wr_out(at_z((2 * direction - 1) * k), "send")
        if k == 4:
            wr_out(at_z(4), "send")

    def wo_share(source):
        block = wo.at[core, source]
        return remote(block, block, s_ws.at[source], r_wo.at[core, source], sibling)

    def wo_forward(source):
        wo_share(source).wait_recv()
        wo_share(source).start()

    def level_of(step_index):
        fraction = jnp.full((8, 128), step_index.astype(F32)) / 1000.0
        return (5.0 * fraction / (1.0 + 4.0 * fraction))[0:1, 0:1]

    levels = (level_of(times[0]), level_of(times[core]))
    shift[0:1, :] = cond[pl.ds(pair[0], 1), :]
    shift[1:2, :] = cond[pl.ds(pair[1 - core], 1), :]
    for load in loads:
        load.wait()

    def mixed(p, rows, cols):
        return (1.0 - levels[p]) * lat[rows, cols].astype(F32) + levels[p] * noi[p, rows, cols].astype(F32)

    for p in range(2):

        @pl.loop(0, TOK // 16)
        def _(b, p=p):
            rows = pl.ds(pl.multiple_of(b * 16, 16), 16)
            total = jnp.zeros((16, DZ), F32)
            for q in range(NZ):
                part = mixed(p, rows, pl.ds(q * DZ, DZ))
                total = total + part * part
            mean = jnp.sum(total, axis=1, keepdims=True) * (1.0 / (NZ * DZ))
            inv[p, rows, :] = lax.rsqrt(mean + EPSILON)

    pl.when(swapped)(begin_ring)

    @pl.when(swapped)
    def _():
        wr_own_remote().start()

    def h_copy(slot):
        return remote(hb.at[0, slot], hb.at[1, slot], s_h.at[slot], r_h.at[slot], partner)

    def distance(i):
        return lax.rem(i + 1, 2) * (-((i + 1) // 2)) + lax.rem(i, 2) * ((i + 1) // 2)

    def make_inputs(first, count):
        @pl.loop(first, first + count)
        def _(i):
            slot = at_z(distance(i))
            cols = pl.ds(pl.multiple_of(slot * DZ, 128), DZ)
            for p in range(2):

                @pl.loop(0, TOK // RB)
                def _(b, p=p):
                    start = pl.multiple_of(b * RB, RB)
                    rows = pl.ds(start, RB)
                    part = mixed(p, rows, cols) * inv[p, rows, :] * gain[:, cols] + shift[p : p + 1, cols]
                    hb[0, slot, pl.ds(p * TOK + start, RB), :] = part.astype(BF16)

            @pl.when(swapped)
            def _():
                h_copy(slot).start()

    acc[...] = jnp.zeros_like(acc)

    def multiply(index, slot):
        for j in range(3):
            from_sibling(index, slot, j).wait_recv()

        @pl.when(swapped)
        def _():
            h_copy(slot).wait_recv()

        @pl.loop(0, 3)
        def _(j):
            acc[j] += jnp.dot(hb[sel, slot], wbuf[slot, j], preferred_element_type=F32)

    groups = [[(0, 0)], [(1, -1), (2, 1)], [(3, -2), (4, 2)], [(5, -3), (6, 3)], [(7, 4)]]
    make_inputs(0, 2)
    for k in range(1, 5):
        if k == 4:
            for index, step in groups[3]:
                multiply(index, at_z(step))
        for j in range(3):
            for direction in range(2):
                landing(direction, k, j).wait_recv()
                if k < 4:
                    ring(direction, k + 1, j).start()
                    index, step = groups[k][direction]
                    to_sibling(index, at_z(step), j).start()
            if k == 4:
                index, step = groups[k][0]
                to_sibling(index, at_z(step), j).start()
            if k == 1:
                make_inputs(2 + 2 * j, 2)
        if k == 3:
            wr_begin()
        if k == 4:
            wr_step(1)
        if k < 4:
            for index, step in groups[k - 1]:
                multiply(index, at_z(step))
    for index, step in groups[4]:
        multiply(index, at_z(step))

    my_part = pl.ds(z * TOK, TOK)

    def unit_remote(u):
        return remote(
            units.at[u], ub.at[:, core, my_part], s_a.at[u], r_a.at[z], {"z": owner_of(u)}
        )

    def unit_local(u):
        return pltpu.make_async_copy(units.at[u], ub.at[:, core, my_part], r_a.at[z])

    for u in range(UNITS):
        p, h = u // 3, u % 3
        for j in range(3):
            units[u, j] = acc[j, p * TOK : (p + 1) * TOK, h * HD : (h + 1) * HD].astype(BF16)

        @pl.when(z == owner_of(u))
        def _(u=u):
            unit_local(u).start()

        @pl.when(z != owner_of(u))
        def _(u=u):
            unit_remote(u).start()

    wr_step(2)
    is_owner = lax.rem(z, 4) != 3
    mine = jnp.minimum(z - z // 4, UNITS - 1)
    mine_rows = pl.ds(pl.multiple_of((mine // 3) * TOK, TOK), TOK)
    mine_cols = pl.ds(pl.multiple_of(lax.rem(mine, 3) * HD, HD), HD)

    def arrived(source):
        block = ub.at[:, core, pl.ds(source * TOK, TOK)]
        return remote(block, block, s_a.at[0], r_a.at[source], sibling)

    def kv_to_sibling(source, which):
        block = ub.at[pl.ds(1, 2), which, pl.ds(source * TOK, TOK)]
        return remote(block, block, s_kv.at[source], r_kv.at[source], sibling)

    def o_remote(to):
        return remote(ob.at[to], att.at[f, mine_rows, mine_cols], s_o.at[to], r_o.at[mine], {"z": to})

    def o_local(to):
        return pltpu.make_async_copy(ob.at[to], att.at[f, mine_rows, mine_cols], r_o.at[mine])

    @pl.when(is_owner)
    def _():
        @pl.loop(0, NZ)
        def _(i):
            source = at_z(distance(i))
            arrived(source).wait_recv()
            kv_to_sibling(source, core).start()

        @pl.loop(0, NZ)
        def _(i):
            kv_to_sibling(at_z(distance(i)), 1 - core).wait_recv()


    wr_step(3)

    @pl.loop(0, NZ)
    def _(i):
        to = at_z(distance(NZ - 1 - i))

        @pl.when(is_owner)
        def _():
            queries = ub[0, core, pl.ds(pl.multiple_of(to * TOK, TOK), TOK), :]
            keys = ub[1].reshape(2 * NZ * TOK, HD)
            scores = lax.dot_general(
                queries, keys, (((1,), (1,)), ((), ())), preferred_element_type=F32
            )
            peak = jnp.max(scores, axis=1, keepdims=True)
            weight = jnp.exp2((scores - peak) * (HD**-0.5 * LOG2E))
            mass = jnp.sum(weight, axis=1, keepdims=True)
            result = jnp.dot(
                weight.astype(BF16), ub[2].reshape(2 * NZ * TOK, HD), preferred_element_type=F32
            )
            ob[to] = (result / mass).astype(BF16)

            @pl.when(to == z)
            def _():
                o_local(to).start()

            @pl.when(to != z)
            def _():
                o_remote(to).start()

        pl.when(i == 3)(functools.partial(wr_step, 4))

    other_f = (1 - y_lo) * 4 + x
    far_f = y_lo * 4 + lax.rem(x + 2, 4)
    x_up, x_down = ({"x": lax.rem(x + step, 4)} for step in (1, 3))
    left_f, right_f = (y_lo * 4 + lax.rem(x + step, 4) for step in (3, 1))
    y_other = {"y_lo": 1 - y_lo}

    def att_copy(lane, source, p, device):
        block = att.at[source, pl.ds(p * TOK, TOK)]
        return remote(block, block, s_att.at[lane, p], r_att.at[source, p], device)

    def att_wait(source, p):
        att_copy(0, source, p, sibling).wait_recv()

    def att_first(p):
        return [
            att_copy(lane, f, p, device) for lane, device in enumerate((y_other, x_up, x_down))
        ]

    def far_half(lane, source, p):
        block = att.at[source, pl.ds(p * TOK + lane * (TOK // 2), TOK // 2)]
        return remote(block, block, s_far.at[lane, p], r_far.at[lane, p], (x_up, x_down)[lane])

    def pass_on(p):
        for lane, source in ((0, left_f), (1, right_f)):
            att_wait(source, p)
            far_half(lane, source, p).start()

    def att_second(p):
        return [att_copy(4, other_f, p, x_up), att_copy(5, other_f, p, x_down)]

    def att_third(p):
        return [att_copy(6, far_f, p, y_other)]

    def first(p):
        for h in range(3):
            block = att.at[f, pl.ds(p * TOK, TOK), pl.ds(h * HD, HD)]
            remote(block, block, s_o.at[0], r_o.at[p * 3 + h], sibling).wait_recv()
        for copy in att_first(p):
            copy.start()

    def second(p):
        att_wait(other_f, p)
        for copy in att_second(p):
            copy.start()

    def third(p):
        for lane in range(2):
            far_half(lane, far_f, p).wait_recv()
        for copy in att_third(p):
            copy.start()

    first(0)
    first(1)
    target_load.wait()
    difference = target[...].astype(F32) - lat[:, window].astype(F32)

    @pl.when(lax.rem(out_block, 2) == 0)
    def _():
        base[...] = difference[:, :ROWS]

    @pl.when(lax.rem(out_block, 2) == 1)
    def _():
        base[...] = difference[:, COLS - ROWS :]

    pass_on(0)
    second(0)
    third(0)

    @pl.loop(0, 8)
    def _(source):
        wo_forward(source)

    pass_on(1)
    second(1)
    third(1)

    def fin_copy(half, p):
        return remote(
            pb.at[half, p], fin.at[y_hi, p], s_f.at[half, p], r_f.at[y_hi, p], {"core": half, "y_hi": core}
        )

    def send_half(half, p):
        stays = (core == half) & (y_hi == core)

        @pl.when(stays)
        def _():
            pltpu.make_async_copy(pb.at[half, p], fin.at[y_hi, p], r_f.at[y_hi, p]).start()

        @pl.when(jnp.logical_not(stays))
        def _():
            fin_copy(half, p).start()

    near = [y_lo * 4 + lax.rem(x + step, 4) for step in (1, 3)]
    across = [(1 - y_lo) * 4 + lax.rem(x + step, 4) for step in (1, 3, 2)]
    for p in range(2):
        rows = pl.ds(p * TOK, TOK)
        for place, source in enumerate([f, other_f, far_f, *near, *across]):
            if place > 4:
                att_wait(source, p)
            if p == 0:
                block = wo.at[1 - core, source]
                remote(block, block, s_ws.at[source], r_wo.at[1 - core, source], sibling).wait_recv()
            for half in range(2):
                product = lax.dot_general(
                    att[source, rows], wo[half, source], (((1,), (1,)), ((), ())), preferred_element_type=F32
                )
                if place == 0:
                    pred[half] = product
                elif place < 7:
                    pred[half] += product
                else:
                    pb[half, p] = (pred[half] + product).astype(BF16)
                    send_half(half, p)

    for p in range(2):
        for section in range(2):
            block = fin.at[section, p]
            remote(block, block, s_f.at[0, p], r_f.at[section, p], sibling).wait_recv()

    def found(section, p):
        return fin[section, p].astype(F32)

    dmd[...] = found(1, 0) - (found(0, 1) + GUIDANCE * (found(0, 0) - found(0, 1)))
    residual[...] = found(1, 1) - base[...]

    @pl.when(swapped)
    def _():
        for j in range(3):
            own_remote(j).wait_send()
        wr_own_remote().wait_send()
        for slot in range(NZ):
            h_copy(slot).wait_send()

    for slot in range(NZ):
        wr_out(slot, "wait")
        wo_share(slot).wait_send()
    for k in range(1, 5):
        for direction in range(2):
            wr_copy(direction, k, 0).wait_send()
    for k in range(1, 5):
        for j in range(3):
            for direction in range(2):
                ring(direction, k, j).wait_send()
    for group in groups:
        for index, step in group:
            for j in range(3):
                to_sibling(index, at_z(step), j).wait_send()
    for u in range(UNITS):

        @pl.when(z != owner_of(u))
        def _(u=u):
            unit_remote(u).wait_send()

    @pl.when(is_owner)
    def _():
        for source in range(NZ):
            kv_to_sibling(source, core).wait_send()

            @pl.when(z != source)
            def _(source=source):
                o_remote(source).wait_send()

    for p in range(2):
        far_half(0, left_f, p).wait_send()
        far_half(1, right_f, p).wait_send()
        for copy in att_first(p) + att_second(p) + att_third(p):
            copy.wait_send()
    for half in range(2):

        @pl.when(jnp.logical_not((core == half) & (y_hi == core)))
        def _(half=half):
            for p in range(2):
                fin_copy(half, p).wait_send()


def outputs(times, pair, latents, noise, cond_table, gain, w_qkv, w_out):
    dma = pltpu.SemaphoreType.DMA
    vmem, any_space = pl.BlockSpec(memory_space=pltpu.VMEM), pl.BlockSpec(memory_space=pl.ANY)
    smem = pl.BlockSpec(memory_space=pltpu.SMEM)
    return pl.pallas_call(
        step_kernel,
        out_shape=[jax.ShapeDtypeStruct((TOK, ROWS), F32)] * 2,
        in_specs=[smem, smem, any_space, any_space, vmem, vmem, any_space, any_space],
        out_specs=[vmem, vmem],
        scratch_shapes=[
            pltpu.VMEM((TOK, NZ * DZ), BF16),
            pltpu.VMEM((2, TOK, NZ * DZ), BF16),
            pltpu.VMEM((2, NZ * DZ), F32),
            pltpu.VMEM((2, NZ, 2 * TOK, DZ), BF16),
            pltpu.VMEM((2, TOK, 1), F32),
            pltpu.VMEM((NZ, 3, DZ, COLS), BF16),
            pltpu.VMEM((3, 2 * TOK, COLS), F32),
            pltpu.VMEM((UNITS, 3, TOK, HD), BF16),
            pltpu.VMEM((3, 2, NZ * TOK, HD), BF16),
            pltpu.VMEM((NZ, TOK, HD), BF16),
            pltpu.VMEM((8, 2 * TOK, COLS), BF16),
            pltpu.VMEM((NZ, ROWS, COLS), BF16),
            pltpu.VMEM((2, 8, ROWS, COLS), BF16),
            pltpu.VMEM((2, TOK, ROWS), F32),
            pltpu.VMEM((2, 2, TOK, ROWS), BF16),
            pltpu.VMEM((2, 2, TOK, ROWS), BF16),
            pltpu.VMEM((TOK, COLS), BF16),
            pltpu.VMEM((TOK, ROWS), F32),
            dma((4,)),
            dma((3,)), dma((3,)),
            dma((NZ,)), dma((NZ,)),
            dma((2, 4, 3)), dma((2, 4, 3)),
            dma((NZ, 3)), dma((NZ, 3)),
            dma((UNITS,)), dma((NZ,)),
            dma((NZ,)), dma((NZ,)),
            dma((NZ,)), dma((UNITS,)),
            dma((2, 5)), dma((2, 5)), dma((NZ,)), dma((2, 8)), dma((8,)),
            dma((7, 2)), dma((8, 2)),
            dma((2, 2)), dma((2, 2)),
            dma((2, 2)), dma((2, 2)),
        ],
        compiler_params=pltpu.CompilerParams(
            collective_id=0, has_side_effects=True, vmem_limit_bytes=60 * 2**20
        ),
        cost_estimate=pl.CostEstimate(
            flops=9_000_000_000, bytes_accessed=40_000_000, transcendentals=5_000_000
        ),
    )(times, pair, latents, noise, cond_table, gain, w_qkv, w_out)


def body(latents, noise, time_index, cfg_pair, cond_table, gain, w_qkv, w_out):
    return tuple(
        outputs(
            time_index, cfg_pair, latents, noise, cond_table, gain, w_qkv, jnp.swapaxes(w_out[0], 0, 1)
        )
    )


def solution(mesh):
    torus = Mesh(mesh.devices.reshape(2, NZ, 2, 2, 4), AXES)
    seq, fsdp = ("z", "y_hi"), ("y_lo", "x")
    return jax.shard_map(
        body,
        mesh=torus,
        in_specs=(
            P(seq, None),
            P(None, seq, None),
            P(),
            P(),
            P(),
            P("core", None),
            P("core", None, seq, fsdp),
            P("core", fsdp, seq),
        ),
        out_specs=(P(seq, ("core", *fsdp)), P(seq, ("core", *fsdp))),
        check_vma=False,
    )
```
